32 devices in a mesh: dp: 2 (over x), section: 4 (over z), seq: 4 (over y, core).
Axes of the slice: x: 2, y: 2, z: 4, core: 2. Of those that a mesh axis runs over, the one named last changes fastest.
Arguments:
- section_inputs: bfloat16 [4, 3, 2, 512, 768], P('section', None, 'dp', 'seq'), may hold values from -6 to 6
- cotangent: bfloat16 [3, 2, 512, 768], P(None, 'dp', 'seq'), may hold values from -6 to 6
- conv_weight: bfloat16 [4, 3, 768, 384], P('section'), may hold values from -0.125 to 0.125
- out_weight: bfloat16 [4, 384, 768], P('section'), may hold values from -0.3125 to 0.3125
- norm_scale: float32 [4, 768], P('section'), may hold values from 0.25 to 1.75
- norm_shift: float32 [4, 768], P('section'), may hold values from -3 to 3
- inner_scale: float32 [4, 384], P('section'), may hold values from 0.25 to 1.75
- inner_shift: float32 [4, 384], P('section'), may hold values from -3 to 3
Outputs:
- grad_in: bfloat16 [4, 3, 2, 512, 768], P('section', None, 'dp', 'seq')
- grad_conv: float32 [4, 3, 768, 384], P('section', None, 'seq')
- grad_out: float32 [4, 384, 768], P('section', None, 'seq')
The draws below stay inside these ranges and needn't reach their ends.
All inputs are finite; a program needn't handle non-finite values.
Results may differ from the reference program's by a relative error of at most 0.025.
Values may be sent and summed in bfloat16 or wider, within the bound.
No kernel may reach another device: no remote copies, remote signals or barrier semaphores. Data moves between devices by JAX's collectives and lax.ppermute only.
A program may use at most 64 MiB of HBM per device.

```python
import jax
import jax.numpy as jnp
from jax import lax

C = 768
I = 384
P_DEV = 128
MICRO = 3
BASE_DILATION = 32
SECTIONS = 4
WINDOWS = 2
LENGTH = 512
N_SEQ = 4


def strengthened(array, rng, source, target, blocks, factor):
    def block_of(axis_at):
        return (jnp.arange(array.shape[axis_at]) // (array.shape[axis_at] // blocks)).reshape((-1,) + (1,) * (array.ndim - 1 - axis_at))

    near = jax.random.permutation(rng, blocks)[block_of(target)]
    other_side = (block_of(target) + blocks // 2) % blocks
    return jnp.where((block_of(source) == near) | (block_of(source) == other_side), factor * array, array)


def levels(own_key, extent, shards, low, top_value):
    level, own = 1.0, jax.random.fold_in(own_key, 6)
    for position, blocks in shards:
        steps = jnp.exp(jax.random.uniform(jax.random.fold_in(own, position), (blocks,), jnp.float32, low / len(shards), top_value / len(shards)))
        level = level * jnp.repeat(steps, extent[position] // blocks).reshape([-1 if axis == position else 1 for axis in range(len(extent))])
    return level


def normal_values(stream_key, dims, width, limit, pieces=(), kind=jnp.bfloat16):
    array = jax.random.normal(stream_key, dims, jnp.float32) * width
    if len(pieces) > 0:
        array = levels(stream_key, dims, pieces, -0.22, 0.18) * array
    return jnp.clip(array, min=-limit, max=limit).astype(kind)


def gaussian_with(own_key, dims, spread, limit, split, heavy, held_as=jnp.bfloat16):
    entries = spread * jax.random.normal(own_key, dims, jnp.float32)
    if split:
        entries = entries * levels(own_key, dims, split, -0.22, 0.18)
    return jnp.clip(strengthened(entries, jax.random.fold_in(own_key, 3), *heavy), -limit, limit).astype(held_as)


def setup_inputs(seed: int = 0) -> dict:
    arg_keys = jax.random.split(jax.random.key(seed), 9)
    return {
        "section_inputs": normal_values(arg_keys[0], (SECTIONS, MICRO, WINDOWS, LENGTH, C), 1.0, 6.0, ((0, 4), (2, 2), (3, 4))),
        "cotangent": gaussian_with(arg_keys[1], (MICRO, WINDOWS, LENGTH, C), 1.0, 6.0, ((1, 2), (2, 4)), (2, 3, 4, 2.0)),
        "conv_weight": normal_values(arg_keys[2], (SECTIONS, 3, C, I), (3 * C) ** -0.5, 0.125, ((0, 4),)),
        "out_weight": normal_values(arg_keys[3], (SECTIONS, I, C), I ** -0.5, 0.3125, ((0, 4),)),
        "norm_scale": jnp.clip(1.0 + 0.15 * jax.random.normal(arg_keys[4], (SECTIONS, C), jnp.float32), 0.25, 1.75),
        "norm_shift": normal_values(arg_keys[5], (SECTIONS, C), 0.5, 3.0, ((0, 4),), jnp.float32),
        "inner_scale": jnp.clip(1.0 + 0.15 * jax.random.normal(arg_keys[6], (SECTIONS, I), jnp.float32), 0.25, 1.75),
        "inner_shift": normal_values(arg_keys[7], (SECTIONS, I), 0.5, 3.0, ((0, 4),), jnp.float32),
    }


gelu_coeff = 0.7978845608028654
cubic_coeff = 0.044715


def gelu_pair(inputs):
    inner_arg = gelu_coeff * (inputs + cubic_coeff * inputs * inputs * inputs)
    tanh_val = jnp.tanh(inner_arg)
    result = 0.5 * inputs * (1.0 + tanh_val)
    slope_val = 0.5 * (1.0 + tanh_val) + 0.5 * inputs * (1.0 - tanh_val * tanh_val) * gelu_coeff * (1.0 + 3.0 * cubic_coeff * inputs * inputs)
    return result, slope_val


def round_trip(values):
    return lax.optimization_barrier(values.astype(jnp.bfloat16)).astype(jnp.float32)


def section_backward(block_in, grad_top, convolution_kernel, out_w, scale_one, shift_one, scale_two, shift_two, dilation_rate):
    channels = block_in.shape[-1]
    inner_width = convolution_kernel.shape[2]
    pre_norm = block_in.astype(jnp.float32) * scale_one + shift_one
    act_val, act_slope = gelu_pair(pre_norm)
    hidden = act_val.astype(jnp.bfloat16)
    padded = jnp.pad(hidden, ((0, 0), (0, 0), (dilation_rate, dilation_rate), (0, 0)))
    tap_rows = jnp.concatenate([padded[:, :, tap_number * dilation_rate: tap_number * dilation_rate + LENGTH] for tap_number in range(3)], axis=3)
    conv_out = jnp.dot(tap_rows.reshape(-1, 3 * channels), convolution_kernel.reshape(3 * channels, inner_width), preferred_element_type=jnp.float32)
    inner_pre = conv_out.reshape(tap_rows.shape[:3] + (inner_width,)) * scale_two + shift_two
    inner_val, inner_slope = gelu_pair(inner_pre)
    inner_act = inner_val.astype(jnp.bfloat16)
    grad_inner = jnp.dot(grad_top.reshape(-1, channels), out_w.T, preferred_element_type=jnp.float32).reshape(inner_pre.shape)
    grad_conv = (grad_inner * inner_slope * scale_two).astype(jnp.bfloat16)
    grad_pad = jnp.pad(grad_conv, ((0, 0), (0, 0), (dilation_rate, dilation_rate), (0, 0)))
    back_taps = jnp.concatenate([grad_pad[:, :, (2 - tap_number) * dilation_rate: (2 - tap_number) * dilation_rate + LENGTH] for tap_number in range(3)], axis=3)
    back_weight = jnp.transpose(convolution_kernel, (0, 2, 1)).reshape(3 * inner_width, channels)
    grad_hidden = jnp.dot(back_taps.reshape(-1, 3 * inner_width), back_weight, preferred_element_type=jnp.float32).reshape(block_in.shape)
    grad_block = (grad_top.astype(jnp.float32) + grad_hidden * act_slope * scale_one).astype(jnp.bfloat16)
    return tap_rows, inner_act, grad_conv, grad_block


def block_partials(tap_rows, inner_act, grad_conv, grad_top):
    def one_block(block_num):
        start = (block_num * P_DEV).astype(jnp.int32)
        taps_blk = lax.dynamic_slice_in_dim(tap_rows, start, P_DEV, 2).astype(jnp.float32)
        conv_blk = lax.dynamic_slice_in_dim(grad_conv, start, P_DEV, 2).astype(jnp.float32)
        act_blk = lax.dynamic_slice_in_dim(inner_act, start, P_DEV, 2).astype(jnp.float32)
        top_blk = lax.dynamic_slice_in_dim(grad_top, start, P_DEV, 2).astype(jnp.float32)
        conv_part = jnp.sum(round_trip(jnp.einsum('mwpa,mwpi->wai', taps_blk, conv_blk)), axis=0)
        out_part = jnp.sum(round_trip(jnp.einsum('mwpi,mwpc->wic', act_blk, top_blk)), axis=0)
        return conv_part, out_part

    conv_parts, out_parts = lax.map(one_block, jnp.arange(N_SEQ, dtype=jnp.int32))
    return jnp.sum(conv_parts, axis=0), jnp.sum(out_parts, axis=0)


def reference(section_inputs, cotangent, conv_weight, out_weight, norm_scale, norm_shift, inner_scale, inner_shift):
    grad_list = [None] * SECTIONS
    conv_list = [None] * SECTIONS
    out_list = [None] * SECTIONS
    grad_top = cotangent
    factor = 1.0 / float(MICRO * WINDOWS)
    for section_total in range(SECTIONS - 1, -1, -1):
        dilation_rate = BASE_DILATION * (1 + section_total % 2)
        tap_rows, inner_act, grad_conv, grad_block = section_backward(section_inputs[section_total], grad_top, conv_weight[section_total], out_weight[section_total], norm_scale[section_total], norm_shift[section_total], inner_scale[section_total], inner_shift[section_total], dilation_rate)
        conv_sum, out_sum = block_partials(tap_rows, inner_act, grad_conv, grad_top)
        conv_list[section_total] = (conv_sum * factor).reshape(3, C, I)
        out_list[section_total] = out_sum * factor
        grad_list[section_total] = grad_block
        grad_top = grad_block
    return jnp.stack(grad_list), jnp.stack(conv_list), jnp.stack(out_list)
```

```python
import jax
import jax.numpy as jnp
from jax import lax
from jax.sharding import PartitionSpec as P

BASE_DILATION = 32
LAG = 2


gelu_coeff = 0.7978845608028654
cubic_coeff = 0.044715


def gelu_pair(inputs):
    squared = inputs * inputs
    inner_arg = gelu_coeff * (inputs + cubic_coeff * inputs * squared)
    tanh_val = jnp.tanh(inner_arg)
    result = 0.5 * inputs * (1.0 + tanh_val)
    slope_val = 0.5 * (1.0 + tanh_val) + 0.5 * inputs * (1.0 - tanh_val * tanh_val) * gelu_coeff * (
        1.0 + 3.0 * cubic_coeff * squared
    )
    return (result, slope_val)


def seq_swap(value, bit):
    count = lax.axis_size("seq")
    return lax.ppermute(value, "seq", [(i, i ^ bit) for i in range(count)])


def dp_swap(value):
    return lax.ppermute(value, "dp", [(0, 1), (1, 0)])


def pick(value, index, axis):
    return lax.dynamic_index_in_dim(value, index, axis, keepdims=False)


def exchange(value, number):
    count = lax.axis_size("seq")
    bit = 1
    while bit < count:
        batch, source, inner, target, rest, channels = value.shape
        split = value.reshape(batch, source, inner, target // 2, 2, rest, channels)
        mine = (number // bit) % 2
        keep = pick(split, mine, 4)
        come = seq_swap(pick(split, 1 - mine, 4), bit)
        first = jnp.where(mine == 0, keep, come)
        second = jnp.where(mine == 0, come, keep)
        value = jnp.stack([first, second], axis=1).reshape(
            batch, 2 * source, inner, target // 2, rest, channels
        )
        bit *= 2
    return value[:, :, :, 0]


def to_residues(value, number):
    batch, rows, channels = value.shape
    count = lax.axis_size("seq")
    value = value.reshape(batch, 1, rows // BASE_DILATION, count, BASE_DILATION // count, channels)
    return exchange(value, number).reshape(batch, rows, channels)


def from_residues(value, number):
    batch, rows, channels = value.shape
    count = lax.axis_size("seq")
    own = BASE_DILATION // count
    inner = rows // BASE_DILATION
    value = value.reshape(batch, 1, count, inner, own, channels).transpose(0, 1, 3, 2, 4, 5)
    value = exchange(value, number)
    return value.transpose(0, 2, 1, 3, 4).reshape(batch, rows, channels)


def shifts(value, step):
    rows = value.shape[-2]
    width = 2 * step[1]
    pad = [(0, 0)] * (value.ndim - 2) + [(width, width), (0, 0)]
    padded = jnp.pad(value, pad)
    axis = value.ndim - 2
    return [
        lax.dynamic_slice_in_dim(padded, width - (tap - 1) * step[0], rows, axis) for tap in range(3)
    ]


def on_device(
    section_inputs,
    cotangent,
    conv_weight,
    out_weight,
    norm_scale,
    norm_shift,
    inner_scale,
    inner_shift,
):
    sections = lax.axis_size("section")
    windows = lax.axis_size("dp")
    count = lax.axis_size("seq")
    section = lax.axis_index("section")
    number = lax.axis_index("seq")
    window = lax.axis_index("dp")
    inputs = section_inputs[0, :, 0]
    top = cotangent[:, 0]
    micro, rows, channels = inputs.shape
    kernel = conv_weight[0]
    inner = kernel.shape[2]
    kernel_flat = kernel.reshape(3 * channels, inner)
    back_kernel = kernel.transpose(0, 2, 1).reshape(3 * inner, channels)
    out_w = out_weight[0]
    own = BASE_DILATION // count
    step = (own * (1 + section % 2), own)
    gathered = count == 4 and windows == 2

    def forward(block_in):
        pre = block_in.astype(jnp.float32) * norm_scale[0] + norm_shift[0]
        act, slope = gelu_pair(pre)
        hidden = act.astype(jnp.bfloat16)
        up, same, down = shifts(hidden, step)
        taps = jnp.concatenate([down, same, up], axis=-1)
        inner_pre = (
            jnp.dot(taps, kernel_flat, preferred_element_type=jnp.float32) * inner_scale[0]
            + inner_shift[0]
        )
        inner_act, inner_slope = gelu_pair(inner_pre)
        return (
            hidden,
            slope * norm_scale[0],
            inner_act.astype(jnp.bfloat16),
            inner_slope * inner_scale[0],
        )

    first = to_residues(jnp.stack([inputs[0], top[0]]), number)
    rest = to_residues(jnp.concatenate([inputs[1:], top[1:]]), number)
    block_in = [first[0]] + [rest[m] for m in range(micro - 1)]
    top = jnp.stack([first[1]] + [rest[micro - 1 + m] for m in range(micro - 1)])
    parts = [forward(one) for one in block_in]
    hidden = [one[0] for one in parts]
    inner_act = [one[2] for one in parts]
    slope = jnp.stack([one[1] for one in parts])
    inner_slope = jnp.stack([one[3] for one in parts])

    if gathered:
        half = channels // 2
        side = number // 2
        wide = jnp.stack(hidden).reshape(micro, rows, 2, half)
        near = jnp.stack([pick(wide, side, 2), seq_swap(pick(wide, 1 - side, 2), 2)])
        far = dp_swap(near)
        hidden_all = jnp.stack(
            [jnp.where(window == 0, near, far), jnp.where(window == 0, far, near)]
        )

    def tick(index, received):
        grad_top = jnp.where(section == sections - 1, pick(top, index, 0), received)
        grad_inner = lax.dot_general(
            grad_top, out_w, (((1,), (1,)), ((), ())), preferred_element_type=jnp.float32
        )
        grad_conv = (grad_inner * pick(inner_slope, index, 0)).astype(jnp.bfloat16)
        back = jnp.concatenate(shifts(grad_conv, step), axis=-1)
        grad_hidden = jnp.dot(back, back_kernel, preferred_element_type=jnp.float32)
        grad_block = (
            grad_top.astype(jnp.float32) + grad_hidden * pick(slope, index, 0)
        ).astype(jnp.bfloat16)
        return grad_top, grad_conv, grad_block

    ticks = micro + LAG * (sections - 1)
    down_pairs = [(i + 1, i) for i in range(sections - 1)]
    sent = []
    done = []
    for number_of in range(ticks):
        index = jnp.clip(number_of - LAG * (sections - 1 - section), 0, micro - 1)
        if number_of == 0:
            index = 0
        received = sent[number_of - LAG] if number_of >= LAG else jnp.zeros_like(top[0])
        result = tick(index, received)
        done.append(result)
        if number_of + LAG < ticks:
            sent.append(lax.ppermute(result[2], "section", down_pairs))

    def of_section(m, which):
        value = done[m][which]
        for below in range(1, sections):
            value = jnp.where(
                section == sections - 1 - below, done[m + LAG * below][which], value
            )
        return value

    grads_out = []
    conv_total = 0.0
    out_part = 0.0
    for m in range(micro):
        grad_top, grad_conv, grad_block = (of_section(m, which) for which in range(3))
        out_part = out_part + lax.dot_general(
            inner_act[m], grad_top, (((0,), (0,)), ((), ())), preferred_element_type=jnp.float32
        )
        if gathered:
            near = jnp.stack([grad_conv, seq_swap(grad_conv, 2)])
            far = dp_swap(near)
            both = jnp.stack(
                [jnp.where(window == 0, near, far), jnp.where(window == 0, far, near)]
            )
            back = jnp.concatenate(shifts(both, step), axis=-1)
            conv_total = conv_total + lax.dot_general(
                hidden_all[:, :, m].reshape(4 * rows, half),
                back.reshape(4 * rows, 3 * inner),
                (((0,), (0,)), ((), ())),
                preferred_element_type=jnp.float32,
            )
        else:
            back = jnp.concatenate(shifts(grad_conv, step), axis=-1)
            conv_total = conv_total + lax.dot_general(
                hidden[m], back, (((0,), (0,)), ((), ())), preferred_element_type=jnp.float32
            )
        grads_out.append(from_residues(grad_block[None], number)[0])

    factor = 1.0 / float(micro * windows)
    if gathered:
        core = number % 2
        share = channels // 4
        split = conv_total.reshape(2, share, 3 * inner)
        come = seq_swap(pick(split, 1 - core, 0).astype(jnp.bfloat16), 1)
        conv_sum = pick(split, core, 0) + come.astype(jnp.float32)
        conv_sum = conv_sum.reshape(share, 3, inner).transpose(1, 0, 2)
        columns = out_part.reshape(inner, 2, 2, share)
        come = seq_swap(pick(columns, 1 - core, 2).astype(jnp.bfloat16), 1)
        columns = pick(columns, core, 2) + come.astype(jnp.float32)
        come = seq_swap(pick(columns, 1 - side, 1).astype(jnp.bfloat16), 2)
        columns = (pick(columns, side, 1) + come.astype(jnp.float32)).astype(jnp.bfloat16)
        out_sum = columns.astype(jnp.float32) + dp_swap(columns).astype(jnp.float32)
    else:
        conv_part = conv_total.reshape(channels, 3, inner).transpose(1, 0, 2)
        conv_sum, out_sum = (
            lax.psum(
                lax.psum_scatter(part.astype(jnp.bfloat16), "seq", scatter_dimension=1, tiled=True),
                "dp",
            ).astype(jnp.float32)
            for part in (conv_part, out_part)
        )
    return (
        jnp.stack(grads_out).reshape(section_inputs.shape),
        (conv_sum * factor)[None],
        (out_sum * factor)[None],
    )


def solution(mesh):
    return jax.shard_map(
        on_device,
        mesh=mesh,
        in_specs=(
            P("section", None, "dp", "seq", None),
            P(None, "dp", "seq", None),
            P("section", None, None, None),
            P("section", None, None),
            P("section", None),
            P("section", None),
            P("section", None),
            P("section", None),
        ),
        out_specs=(
            P("section", None, "dp", "seq", None),
            P("section", None, "seq", None),
            P("section", None, "seq"),
        ),
        check_vma=False,
    )
```

```python
import jax
import jax.numpy as jnp
from jax import lax
from jax.experimental import pallas as pl
from jax.sharding import PartitionSpec as P

BASE_DILATION = 32
LAG = 2


gelu_coeff = 0.7978845608028654
cubic_coeff = 0.044715


def gelu_pair(inputs):
    squared = inputs * inputs
    inner_arg = gelu_coeff * (inputs + cubic_coeff * inputs * squared)
    tanh_val = jnp.tanh(inner_arg)
    result = 0.5 * inputs * (1.0 + tanh_val)
    slope_val = 0.5 * (1.0 + tanh_val) + 0.5 * inputs * (1.0 - tanh_val * tanh_val) * gelu_coeff * (
        1.0 + 3.0 * cubic_coeff * squared
    )
    return (result, slope_val)


def seq_swap(value, bit):
    count = lax.axis_size("seq")
    return lax.ppermute(value, "seq", [(i, i ^ bit) for i in range(count)])


def dp_swap(value):
    return lax.ppermute(value, "dp", [(0, 1), (1, 0)])


def pick(value, index, axis):
    return lax.dynamic_index_in_dim(value, index, axis, keepdims=False)


def exchange(value, number):
    count = lax.axis_size("seq")
    bit = 1
    while bit < count:
        batch, source, inner, target, rest, channels = value.shape
        split = value.reshape(batch, source, inner, target // 2, 2, rest, channels)
        mine = (number // bit) % 2
        keep = pick(split, mine, 4)
        come = seq_swap(pick(split, 1 - mine, 4), bit)
        first = jnp.where(mine == 0, keep, come)
        second = jnp.where(mine == 0, come, keep)
        value = jnp.stack([first, second], axis=1).reshape(
            batch, 2 * source, inner, target // 2, rest, channels
        )
        bit *= 2
    return value[:, :, :, 0]


def to_residues(value, number):
    batch, rows, channels = value.shape
    count = lax.axis_size("seq")
    value = value.reshape(batch, 1, rows // BASE_DILATION, count, BASE_DILATION // count, channels)
    return exchange(value, number).reshape(batch, rows, channels)


def from_residues(value, number):
    batch, rows, channels = value.shape
    count = lax.axis_size("seq")
    own = BASE_DILATION // count
    inner = rows // BASE_DILATION
    value = value.reshape(batch, 1, count, inner, own, channels).transpose(0, 1, 3, 2, 4, 5)
    value = exchange(value, number)
    return value.transpose(0, 2, 1, 3, 4).reshape(batch, rows, channels)


def shifts(value, step):
    rows = value.shape[-2]
    width = 2 * step[1]
    pad = [(0, 0)] * (value.ndim - 2) + [(width, width), (0, 0)]
    padded = jnp.pad(value, pad)
    axis = value.ndim - 2
    return [
        lax.dynamic_slice_in_dim(padded, width - (tap - 1) * step[0], rows, axis) for tap in range(3)
    ]


def passed(value):
    def kernel(value_ref, out_ref):
        out_ref[...] = value_ref[...]

    return pl.pallas_call(kernel, out_shape=jax.ShapeDtypeStruct(value.shape, value.dtype))(value)


def after(value, *events):
    return lax.optimization_barrier((value,) + events)[0]


def choose(flag, first, second):
    return jnp.where(flag, first, second)


def on_device(
    section_inputs,
    cotangent,
    conv_weight,
    out_weight,
    norm_scale,
    norm_shift,
    inner_scale,
    inner_shift,
):
    norm_scale = passed(norm_scale)
    sections = lax.axis_size("section")
    windows = lax.axis_size("dp")
    count = lax.axis_size("seq")
    section = lax.axis_index("section")
    number = lax.axis_index("seq")
    window = lax.axis_index("dp")
    inputs = section_inputs[0, :, 0]
    top = cotangent[:, 0]
    micro, rows, channels = inputs.shape
    kernel = conv_weight[0]
    inner = kernel.shape[2]
    kernel_flat = kernel.reshape(3 * channels, inner)
    back_kernel = kernel.transpose(0, 2, 1).reshape(3 * inner, channels)
    out_w = out_weight[0]
    own = BASE_DILATION // count
    step = (own * (1 + section % 2), own)
    gathered = count == 4 and windows == 2
    core, side = number % 2, number // 2
    ticks = micro + LAG * (sections - 1)
    down_pairs = [(i + 1, i) for i in range(sections - 1)]

    def forward(block_in):
        pre = block_in.astype(jnp.float32) * norm_scale[0] + norm_shift[0]
        act, slope = gelu_pair(pre)
        hidden = act.astype(jnp.bfloat16)
        up, same, down = shifts(hidden, step)
        taps = jnp.concatenate([down, same, up], axis=-1)
        inner_pre = (
            jnp.dot(taps, kernel_flat, preferred_element_type=jnp.float32) * inner_scale[0]
            + inner_shift[0]
        )
        inner_act, inner_slope = gelu_pair(inner_pre)
        return lax.optimization_barrier(
            (
                hidden,
                slope * norm_scale[0],
                inner_act.astype(jnp.bfloat16),
                inner_slope * inner_scale[0],
            )
        )

    both_in = jnp.concatenate([inputs, top])
    if count == 4:
        blocks = both_in.reshape(2 * micro, rows // BASE_DILATION, 2, 2, own, channels)
        keep = pick(blocks, core, 3)
        come = seq_swap(pick(blocks, 1 - core, 3), 1)
        halves = jnp.stack([choose(core == 0, keep, come), choose(core == 0, come, keep)], 1)
        sends, keeps = [], []
        for m in range(micro):
            pair = jnp.stack([halves[m], halves[micro + m]])
            sends.append(pick(pair, 1 - side, 3))
            keeps.append(pick(pair, side, 3))
        comes = [seq_swap(one, 2) for one in sends]

        def arrived(m, *events):
            keep = keeps[m]
            come = after(comes[m], *events)
            pair = jnp.stack([choose(side == 0, keep, come), choose(side == 0, come, keep)], 1)
            return pair[0].reshape(rows, channels), pair[1].reshape(rows, channels)
    else:
        swapped = to_residues(both_in, number)

        def arrived(m, *events):
            return swapped[m], swapped[micro + m]

    tops, hidden, slope, inner_act, inner_slope = [], [], [], [], []

    def tick(index, received):
        def of_index(values):
            value = values[0]
            for m in range(1, len(values)):
                value = jnp.where(index >= m, values[m], value)
            return value

        grad_top = of_index(tops)
        if received is not None:
            grad_top = jnp.where(section == sections - 1, grad_top, received)
        grad_inner = lax.dot_general(
            grad_top, out_w, (((1,), (1,)), ((), ())), preferred_element_type=jnp.float32
        )
        grad_conv = (grad_inner * of_index(inner_slope)).astype(jnp.bfloat16)
        back = jnp.concatenate(shifts(grad_conv, step), axis=-1)
        grad_hidden = jnp.dot(back, back_kernel, preferred_element_type=jnp.float32)
        grad_block = (grad_top.astype(jnp.float32) + grad_hidden * of_index(slope)).astype(
            jnp.bfloat16
        )
        return lax.optimization_barrier((grad_top, grad_conv, grad_block))

    def of_section(m, which):
        value = done[m][which]
        for below in range(1, sections):
            value = jnp.where(
                section == sections - 1 - below, done[m + LAG * below][which], value
            )
        return value

    def exchange_rows(value, far_value):
        return jnp.concatenate(
            [choose(window == 0, value, far_value), choose(window == 0, far_value, value)]
        )

    half = channels // 2
    share = half // 2
    sent, done = [], []
    near_hidden = far_hidden = None
    near_grad, far_grad = [None] * micro, [None] * micro
    back_half = [None] * micro
    conv_total = 0.0
    out_part = 0.0
    for now in range(ticks):
        if now < micro:
            block_in, one_top = arrived(now, *([done[now - 1]] if now else []))
            one = forward(block_in)
            tops.append(one_top)
            hidden.append(one[0])
            slope.append(one[1])
            inner_act.append(one[2])
            inner_slope.append(one[3])
        received = sent[now - LAG] if now >= LAG else None
        if received is not None:
            received = after(received, done[now - 1])
        done.append(tick(now - LAG * (sections - 1 - section), received))
        if now + LAG < ticks:
            sent.append(lax.ppermute(done[now][2], "section", down_pairs))
        if gathered and now == micro:
            wide = jnp.concatenate(hidden)
            mine = choose(side == 0, wide[:, :half], wide[:, half:])
            other = choose(side == 0, wide[:, half:], wide[:, :half])
            mine, other = after((mine, other), done[now])
            near_hidden = (mine, seq_swap(other, 2))
        if gathered and now == micro + 2:
            near_hidden = after(near_hidden, done[now])
            near_hidden = jnp.concatenate(
                [one.reshape(micro, rows, half) for one in near_hidden], axis=1
            )
            far_hidden = dp_swap(near_hidden)
        m = now - LAG * (sections - 1)
        if m >= 0:
            grad_conv = of_section(m, 1)
            if gathered:
                near_grad[m] = (grad_conv, seq_swap(grad_conv, 2))
        if gathered and m >= 1:
            near_grad[m - 1] = jnp.concatenate(after(near_grad[m - 1], done[now]))
            far_grad[m - 1] = dp_swap(near_grad[m - 1])

    if gathered:
        near_grad[-1] = jnp.concatenate(near_grad[-1])
        far_grad[-1] = dp_swap(near_grad[-1])
    for m in range(micro):
        out_part = out_part + lax.dot_general(
            inner_act[m],
            of_section(m, 0),
            (((0,), (0,)), ((), ())),
            preferred_element_type=jnp.float32,
        )
    if gathered:
        halves = [out_part[:, :half], out_part[:, half:]]
        quarters = [[one[:, :share], one[:, share:]] for one in halves]
        send = [choose(core == 0, one[1], one[0]).astype(jnp.bfloat16) for one in quarters]
        keep = [choose(core == 0, one[0], one[1]) for one in quarters]
        come = seq_swap(jnp.stack(send), 1).astype(jnp.float32)
        columns = [keep[0] + come[0], keep[1] + come[1]]
        send = choose(side == 0, columns[1], columns[0]).astype(jnp.bfloat16)
        keep = choose(side == 0, columns[0], columns[1])
        come = seq_swap(send, 2)
        columns = (keep + come.astype(jnp.float32)).astype(jnp.bfloat16)
        out_sum = columns.astype(jnp.float32) + dp_swap(columns).astype(jnp.float32)
    grads_out = [from_residues(of_section(m, 2)[None], number)[0] for m in range(micro)]
    for m in range(micro):
        if gathered:
            all_hidden = exchange_rows(near_hidden[m], far_hidden[m])
            all_grad = exchange_rows(near_grad[m], far_grad[m]).reshape(4, rows, inner)
            back = jnp.concatenate(shifts(all_grad, step), axis=-1).reshape(4 * rows, 3 * inner)
        else:
            all_hidden = hidden[m]
            back = jnp.concatenate(shifts(of_section(m, 1), step), axis=-1)
        conv_total = conv_total + lax.dot_general(
            all_hidden, back, (((0,), (0,)), ((), ())), preferred_element_type=jnp.float32
        )

    factor = 1.0 / float(micro * windows)
    if gathered:
        low, high = conv_total[:share], conv_total[share:]
        come = seq_swap(choose(core == 0, high, low).astype(jnp.bfloat16), 1)
        conv_sum = choose(core == 0, low, high) + come.astype(jnp.float32)
        conv_sum = jnp.stack([conv_sum[:, k * inner : (k + 1) * inner] for k in range(3)])
    else:
        conv_part = conv_total.reshape(channels, 3, inner).transpose(1, 0, 2)
        conv_sum, out_sum = (
            lax.psum(
                lax.psum_scatter(part.astype(jnp.bfloat16), "seq", scatter_dimension=1, tiled=True),
                "dp",
            ).astype(jnp.float32)
            for part in (conv_part, out_part)
        )
    return (
        jnp.stack(grads_out).reshape(section_inputs.shape),
        (conv_sum * factor)[None],
        (out_sum * factor)[None],
    )


def solution(mesh):
    return jax.shard_map(
        on_device,
        mesh=mesh,
        in_specs=(
            P("section", None, "dp", "seq", None),
            P(None, "dp", "seq", None),
            P("section", None, None, None),
            P("section", None, None),
            P("section", None),
            P("section", None),
            P("section", None),
            P("section", None),
        ),
        out_specs=(
            P("section", None, "dp", "seq", None),
            P("section", None, "seq", None),
            P("section", None, "seq"),
        ),
        check_vma=False,
    )
```

```python
import jax
import jax.numpy as jnp
from jax import lax
from jax.experimental import pallas as pl
from jax.experimental.pallas import tpu as pltpu
from jax.sharding import PartitionSpec as P

BASE_DILATION = 32
LAG = 2


gelu_coeff = 0.7978845608028654
cubic_coeff = 0.044715


def gelu_pair(inputs):
    squared = inputs * inputs
    inner_arg = gelu_coeff * (inputs + cubic_coeff * inputs * squared)
    tanh_val = jnp.tanh(inner_arg)
    result = 0.5 * inputs * (1.0 + tanh_val)
    slope_val = 0.5 * (1.0 + tanh_val) + 0.5 * inputs * (1.0 - tanh_val * tanh_val) * gelu_coeff * (
        1.0 + 3.0 * cubic_coeff * squared
    )
    return (result, slope_val)


def seq_swap(value, bit):
    count = lax.axis_size("seq")
    return lax.ppermute(value, "seq", [(i, i ^ bit) for i in range(count)])


def dp_swap(value):
    return lax.ppermute(value, "dp", [(0, 1), (1, 0)])


def pick(value, index, axis):
    return lax.dynamic_index_in_dim(value, index, axis, keepdims=False)


def exchange(value, number):
    count = lax.axis_size("seq")
    bit = 1
    while bit < count:
        batch, source, inner, target, rest, channels = value.shape
        split = value.reshape(batch, source, inner, target // 2, 2, rest, channels)
        mine = (number // bit) % 2
        keep = pick(split, mine, 4)
        come = seq_swap(pick(split, 1 - mine, 4), bit)
        first = jnp.where(mine == 0, keep, come)
        second = jnp.where(mine == 0, come, keep)
        value = jnp.stack([first, second], axis=1).reshape(
            batch, 2 * source, inner, target // 2, rest, channels
        )
        bit *= 2
    return value[:, :, :, 0]


def to_residues(value, number):
    batch, rows, channels = value.shape
    count = lax.axis_size("seq")
    value = value.reshape(batch, 1, rows // BASE_DILATION, count, BASE_DILATION // count, channels)
    return exchange(value, number).reshape(batch, rows, channels)


def from_residues(value, number):
    batch, rows, channels = value.shape
    count = lax.axis_size("seq")
    own = BASE_DILATION // count
    inner = rows // BASE_DILATION
    value = value.reshape(batch, 1, count, inner, own, channels).transpose(0, 1, 3, 2, 4, 5)
    value = exchange(value, number)
    return value.transpose(0, 2, 1, 3, 4).reshape(batch, rows, channels)


def shifts(value, step):
    rows = value.shape[-2]
    width = 2 * step[1]
    pad = [(0, 0)] * (value.ndim - 2) + [(width, width), (0, 0)]
    padded = jnp.pad(value, pad)
    axis = value.ndim - 2
    return [
        lax.dynamic_slice_in_dim(padded, width - (tap - 1) * step[0], rows, axis) for tap in range(3)
    ]


def split_cores(section_inputs, cotangent, core, first, batch):
    rows, channels = cotangent.shape[2:]
    quarter = rows // 4
    blocks = rows // BASE_DILATION

    def kernel(core_ref, inputs_ref, top_ref, send_ref, keep_ref):
        low = core_ref[0] == 0
        for which, value in enumerate((inputs_ref[0, 0, 0], top_ref[0, 0])):
            value = value.astype(jnp.float32).reshape(blocks, 4, quarter // blocks, channels)
            for side in range(2):
                first_part = value[:, 2 * side].reshape(quarter, channels)
                second_part = value[:, 2 * side + 1].reshape(quarter, channels)
                keep = jnp.where(low, first_part, second_part)
                send = jnp.where(low, second_part, first_part)
                keep_ref[which, side] = keep.astype(keep_ref.dtype)
                send_ref[which, side] = send.astype(send_ref.dtype)

    out = jax.ShapeDtypeStruct((2 * batch, 2, quarter, channels), cotangent.dtype)
    part = pl.BlockSpec((2, 2, quarter, channels), lambda m: (m, 0, 0, 0))
    return pl.pallas_call(
        kernel,
        grid=(batch,),
        in_specs=[
            pl.BlockSpec(memory_space=pltpu.SMEM),
            pl.BlockSpec((1, 1, 1, rows, channels), lambda m: (0, first + m, 0, 0, 0)),
            pl.BlockSpec((1, 1, rows, channels), lambda m: (first + m, 0, 0, 0)),
        ],
        out_specs=[part, part],
        out_shape=[out, out],
        compiler_params=pltpu.CompilerParams(vmem_limit_bytes=16 * 2**20),
        cost_estimate=pl.CostEstimate(
            flops=0, bytes_accessed=8 * batch * rows * channels, transcendentals=0
        ),
    )(core.reshape(1).astype(jnp.int32), section_inputs, cotangent)


def after(value, *events):
    return lax.optimization_barrier((value,) + events)[0]


def choose(flag, first, second):
    return jnp.where(flag, first, second)


def on_device(
    section_inputs,
    cotangent,
    conv_weight,
    out_weight,
    norm_scale,
    norm_shift,
    inner_scale,
    inner_shift,
):
    sections = lax.axis_size("section")
    windows = lax.axis_size("dp")
    count = lax.axis_size("seq")
    section = lax.axis_index("section")
    number = lax.axis_index("seq")
    window = lax.axis_index("dp")
    inputs = section_inputs[0, :, 0]
    top = cotangent[:, 0]
    micro, rows, channels = inputs.shape
    kernel = conv_weight[0]
    inner = kernel.shape[2]
    kernel_flat = kernel.reshape(3 * channels, inner)
    out_w = out_weight[0]
    own = BASE_DILATION // count
    step = (own * (1 + section % 2), own)
    gathered = count == 4 and windows == 2
    core, side = number % 2, number // 2
    ticks = micro + LAG * (sections - 1)

    def send_down(value, now):
        return {
            hop: lax.ppermute(value, "section", [(sections - 1 - hop, sections - 2 - hop)])
            for hop in range(sections - 1)
            if 0 <= now - LAG * hop < micro
        }

    def receive(comes, *events):
        value = None
        for hop, come in comes.items():
            come = after(come, *events)
            value = come if value is None else jnp.where(section == sections - 2 - hop, come, value)
        return value

    def forward(block_in):
        pre = block_in.astype(jnp.float32) * norm_scale[0] + norm_shift[0]
        act, slope = gelu_pair(pre)
        hidden = act.astype(jnp.bfloat16)
        up, same, down = shifts(hidden, step)
        taps = jnp.concatenate([down, same, up], axis=-1)
        inner_pre = (
            jnp.dot(taps, kernel_flat, preferred_element_type=jnp.float32) * inner_scale[0]
            + inner_shift[0]
        )
        inner_act, inner_slope = gelu_pair(inner_pre)
        return lax.optimization_barrier(
            (
                hidden,
                slope * norm_scale[0],
                inner_act.astype(jnp.bfloat16),
                inner_slope * inner_scale[0],
            )
        )

    if count == 4:

        def swap_sides(keep, come):
            send = jnp.stack([pick(keep, 1 - side, 1), pick(come, 1 - side, 1)], 1)
            mine = jnp.stack([pick(keep, side, 1), pick(come, side, 1)], 1)
            return send, mine

        def settle(mine, come):
            mine, come = (
                jnp.stack(
                    [
                        choose(core == 0, one[:, 0], one[:, 1]),
                        choose(core == 0, one[:, 1], one[:, 0]),
                    ],
                    1,
                )
                for one in (mine, come)
            )
            both = jnp.stack([choose(side == 0, mine, come), choose(side == 0, come, mine)], 1)
            both = both.reshape(-1, rows, channels)
            return both[0], both[1]

        send, keep = split_cores(section_inputs, cotangent, core, 0, 1)
        come = seq_swap(send, 1)
        later_core = after(core, send)
        later_send, later_keep = split_cores(section_inputs, cotangent, later_core, 1, micro - 1)
        later_come = seq_swap(later_send, 1)
        send, mine = swap_sides(keep, come)
        come = seq_swap(send, 2)
        later_keep = after(later_keep, send)
        later_send, later_mine = swap_sides(later_keep, later_come)
        first_send = send
        parts = [later_send[2 * m : 2 * m + 2] for m in range(micro - 1)]
        parts = lax.optimization_barrier(tuple(parts) + (later_mine,))
        later_mine = parts[-1]
        come = after(come, *parts)
        arriving = [(mine, come)]

        def arrived(m, *events):
            mine, come = arriving[m]
            if m + 1 < micro:
                send = parts[m] if m == 0 else after(parts[m], *events)
                arriving.append((later_mine[2 * m : 2 * m + 2], seq_swap(send, 2)))
            return settle(mine, after(come, *events))
    else:
        swapped = to_residues(jnp.concatenate([inputs, top]), number)
        first_send = swapped

        def arrived(m, *events):
            return swapped[m], swapped[micro + m]

    unit = after(jnp.eye(inner, dtype=jnp.bfloat16), first_send)
    back_kernel = lax.optimization_barrier(
        jnp.concatenate(
            [
                lax.dot_general(
                    unit, kernel[tap], (((1,), (1,)), ((), ())), preferred_element_type=jnp.float32
                ).astype(jnp.bfloat16)
                for tap in range(3)
            ]
        )
    )
    tops, hidden, slope, inner_act, inner_slope = [], [], [], [], []

    def tick(index, received):
        def of_index(values):
            value = values[0]
            for m in range(1, len(values)):
                value = jnp.where(index >= m, values[m], value)
            return value

        grad_top = of_index(tops)
        if received is not None:
            grad_top = jnp.where(section == sections - 1, grad_top, received)
        grad_inner = lax.dot_general(
            grad_top, out_w, (((1,), (1,)), ((), ())), preferred_element_type=jnp.float32
        )
        grad_conv = (grad_inner * of_index(inner_slope)).astype(jnp.bfloat16)
        back = jnp.concatenate(shifts(grad_conv, step), axis=-1)
        grad_hidden = jnp.dot(back, back_kernel, preferred_element_type=jnp.float32)
        grad_block = (grad_top.astype(jnp.float32) + grad_hidden * of_index(slope)).astype(
            jnp.bfloat16
        )
        return lax.optimization_barrier((grad_top, grad_conv, grad_block))

    def of_section(m, which):
        value = done[m][which]
        for below in range(1, sections):
            value = jnp.where(
                section == sections - 1 - below, done[m + LAG * below][which], value
            )
        return value

    def exchange_rows(value, far_value):
        return jnp.concatenate(
            [choose(window == 0, value, far_value), choose(window == 0, far_value, value)]
        )

    half = channels // 2
    share = half // 2
    sent, done = [], []
    near_hidden, far_hidden = [], []
    near_grad, far_grad = [None] * micro, [None] * micro
    conv_total = 0.0
    out_part = 0.0
    for now in range(ticks):
        if now < micro:
            block_in, one_top = arrived(now, *([done[now - 1]] if now else []))
            one = forward(block_in)
            tops.append(one_top)
            hidden.append(one[0])
            slope.append(one[1])
            inner_act.append(one[2])
            inner_slope.append(one[3])
        received = None
        if now >= LAG:
            events = [done[now - 1]]
            if gathered and now == micro + 2:
                events.append(near_hidden)
            if gathered and now == ticks - 2:
                events.append(far_hidden)
            if gathered and now - LAG * (sections - 1) >= 1:
                events.append(near_grad[now - LAG * (sections - 1) - 1])
            received = receive(sent[now - LAG], *events)
        done.append(tick(now - LAG * (sections - 1 - section), received))
        if now + LAG < ticks:
            sent.append(send_down(done[now][2], now))
        if gathered and now == micro - 1:
            wide = jnp.concatenate(after(tuple(hidden), done[now]))
            mine = choose(side == 0, wide[:, :half], wide[:, half:])
            other = choose(side == 0, wide[:, half:], wide[:, :half])
            near_hidden = (mine, seq_swap(other, 2))
        if gathered and now == micro:
            near_hidden = jnp.concatenate(
                [one.reshape(micro, rows, half) for one in after(near_hidden, done[now])], axis=1
            )
            far_hidden = dp_swap(near_hidden)
        m = now - LAG * (sections - 1)
        if m >= 0:
            out_part = out_part + lax.dot_general(
                of_section(m, 0),
                inner_act[m],
                (((0,), (0,)), ((), ())),
                preferred_element_type=jnp.float32,
            )
        if gathered and m >= 0:
            grad_conv = of_section(m, 1)
            near_grad[m] = (grad_conv, seq_swap(grad_conv, 2))
        if gathered and m >= 1:
            near_grad[m - 1] = jnp.concatenate(after(near_grad[m - 1], done[now - 1]))
            far_grad[m - 1] = dp_swap(near_grad[m - 1])

    def add_conv(total, m, *events):
        if gathered:
            all_hidden = exchange_rows(near_hidden[m], far_hidden[m])
            all_grad = exchange_rows(near_grad[m], after(far_grad[m], *events))
            all_grad = all_grad.reshape(4, rows, inner)
            back = jnp.concatenate(shifts(all_grad, step), axis=-1).reshape(4 * rows, 3 * inner)
        else:
            all_hidden = hidden[m]
            back = jnp.concatenate(shifts(of_section(m, 1), step), axis=-1)
        return total + lax.dot_general(
            all_hidden, back, (((0,), (0,)), ((), ())), preferred_element_type=jnp.float32
        )

    if gathered:
        quarters = out_part.reshape(2, 2, share, inner)
        keep = choose(core == 0, quarters[:, 0], quarters[:, 1])
        send = choose(core == 0, quarters[:, 1], quarters[:, 0]).astype(jnp.bfloat16)
        come_out = seq_swap(send, 1)
        far_grad[-2] = after(far_grad[-2], send)
        near_grad[-1] = jnp.concatenate(after(near_grad[-1], far_grad[-2]))
        far_grad[-1] = dp_swap(near_grad[-1])
        come_out = after(come_out, near_grad[-1]).astype(jnp.float32)
        columns = [keep[0] + come_out[0], keep[1] + come_out[1]]
        send = choose(side == 0, columns[1], columns[0]).astype(jnp.bfloat16)
        keep = choose(side == 0, columns[0], columns[1])
        come = seq_swap(send, 2)
        grads = jnp.stack([of_section(m, 2) for m in range(micro)])
        grads_out = from_residues(after(grads, send), number)
        for m in range(micro - 1):
            conv_total = lax.optimization_barrier(add_conv(conv_total, m, send))
        come = after(come, conv_total)
        columns = (keep + come.astype(jnp.float32)).astype(jnp.bfloat16)
        come_out = dp_swap(columns)
        conv_total = add_conv(conv_total, micro - 1, columns)
        out_sum = (columns.astype(jnp.float32) + come_out.astype(jnp.float32)).T
    else:
        for m in range(micro):
            conv_total = add_conv(conv_total, m)
        grads_out = from_residues(jnp.stack([of_section(m, 2) for m in range(micro)]), number)

    factor = 1.0 / float(micro * windows)
    if gathered:
        low, high = conv_total[:share], conv_total[share:]
        come = seq_swap(choose(core == 0, high, low).astype(jnp.bfloat16), 1)
        conv_sum = choose(core == 0, low, high) + come.astype(jnp.float32)
        conv_sum = jnp.stack([conv_sum[:, k * inner : (k + 1) * inner] for k in range(3)])
    else:
        out_part = out_part.T
        conv_part = conv_total.reshape(channels, 3, inner).transpose(1, 0, 2)
        conv_sum, out_sum = (
            lax.psum(
                lax.psum_scatter(part.astype(jnp.bfloat16), "seq", scatter_dimension=1, tiled=True),
                "dp",
            ).astype(jnp.float32)
            for part in (conv_part, out_part)
        )
    return (
        grads_out.reshape(section_inputs.shape),
        (conv_sum * factor)[None],
        (out_sum * factor)[None],
    )


def solution(mesh):
    return jax.shard_map(
        on_device,
        mesh=mesh,
        in_specs=(
            P("section", None, "dp", "seq", None),
            P(None, "dp", "seq", None),
            P("section", None, None, None),
            P("section", None, None),
            P("section", None),
            P("section", None),
            P("section", None),
            P("section", None),
        ),
        out_specs=(
            P("section", None, "dp", "seq", None),
            P("section", None, "seq", None),
            P("section", None, "seq"),
        ),
        check_vma=False,
    )
```

```python
import jax
import jax.numpy as jnp
from jax import lax
from jax.experimental import pallas as pl
from jax.experimental.pallas import tpu as pltpu
from jax.sharding import PartitionSpec as P

BASE_DILATION = 32
LAG = 2
NEAR = 5
FAR = 8


gelu_coeff = 0.7978845608028654
cubic_coeff = 0.044715


def gelu_pair(inputs):
    squared = inputs * inputs
    inner_arg = gelu_coeff * (inputs + cubic_coeff * inputs * squared)
    tanh_val = jnp.tanh(inner_arg)
    result = 0.5 * inputs * (1.0 + tanh_val)
    slope_val = 0.5 * (1.0 + tanh_val) + 0.5 * inputs * (1.0 - tanh_val * tanh_val) * gelu_coeff * (
        1.0 + 3.0 * cubic_coeff * squared
    )
    return (result, slope_val)


def seq_swap(value, bit):
    count = lax.axis_size("seq")
    return lax.ppermute(value, "seq", [(i, i ^ bit) for i in range(count)])


def dp_swap(value):
    return lax.ppermute(value, "dp", [(0, 1), (1, 0)])


def pick(value, index, axis):
    return lax.dynamic_index_in_dim(value, index, axis, keepdims=False)


def exchange(value, number):
    count = lax.axis_size("seq")
    bit = 1
    while bit < count:
        batch, source, inner, target, rest, channels = value.shape
        split = value.reshape(batch, source, inner, target // 2, 2, rest, channels)
        mine = (number // bit) % 2
        keep = pick(split, mine, 4)
        come = seq_swap(pick(split, 1 - mine, 4), bit)
        first = jnp.where(mine == 0, keep, come)
        second = jnp.where(mine == 0, come, keep)
        value = jnp.stack([first, second], axis=1).reshape(
            batch, 2 * source, inner, target // 2, rest, channels
        )
        bit *= 2
    return value[:, :, :, 0], come


def to_residues(value, number):
    batch, rows, channels = value.shape
    count = lax.axis_size("seq")
    value = value.reshape(batch, 1, rows // BASE_DILATION, count, BASE_DILATION // count, channels)
    return exchange(value, number)[0].reshape(batch, rows, channels)


def from_residues(value, number):
    batch, rows, channels = value.shape
    count = lax.axis_size("seq")
    own = BASE_DILATION // count
    inner = rows // BASE_DILATION
    value = value.reshape(batch, 1, count, inner, own, channels).transpose(0, 1, 3, 2, 4, 5)
    value, come = exchange(value, number)
    return value.transpose(0, 2, 1, 3, 4).reshape(batch, rows, channels), come


def shifts(value, step):
    rows = value.shape[-2]
    width = 2 * step[1]
    pad = [(0, 0)] * (value.ndim - 2) + [(width, width), (0, 0)]
    padded = jnp.pad(value, pad)
    axis = value.ndim - 2
    return [
        lax.dynamic_slice_in_dim(padded, width - (tap - 1) * step[0], rows, axis) for tap in range(3)
    ]


def split_cores(section_inputs, cotangent, core, first, batch):
    rows, channels = cotangent.shape[2:]
    quarter = rows // 4
    blocks = rows // BASE_DILATION

    def kernel(core_ref, inputs_ref, top_ref, send_ref, keep_ref):
        low = core_ref[0] == 0
        for which, value in enumerate((inputs_ref[0, 0, 0], top_ref[0, 0])):
            value = value.astype(jnp.float32).reshape(blocks, 4, quarter // blocks, channels)
            for side in range(2):
                first_part = value[:, 2 * side].reshape(quarter, channels)
                second_part = value[:, 2 * side + 1].reshape(quarter, channels)
                keep = jnp.where(low, first_part, second_part)
                send = jnp.where(low, second_part, first_part)
                keep_ref[which, side] = keep.astype(keep_ref.dtype)
                send_ref[which, side] = send.astype(send_ref.dtype)

    out = jax.ShapeDtypeStruct((2 * batch, 2, quarter, channels), cotangent.dtype)
    part = pl.BlockSpec((2, 2, quarter, channels), lambda m: (m, 0, 0, 0))
    return pl.pallas_call(
        kernel,
        grid=(batch,),
        in_specs=[
            pl.BlockSpec(memory_space=pltpu.SMEM),
            pl.BlockSpec((1, 1, 1, rows, channels), lambda m: (0, first + m, 0, 0, 0)),
            pl.BlockSpec((1, 1, rows, channels), lambda m: (first + m, 0, 0, 0)),
        ],
        out_specs=[part, part],
        out_shape=[out, out],
        compiler_params=pltpu.CompilerParams(vmem_limit_bytes=16 * 2**20),
        cost_estimate=pl.CostEstimate(
            flops=0, bytes_accessed=8 * batch * rows * channels, transcendentals=0
        ),
    )(core.reshape(1).astype(jnp.int32), section_inputs, cotangent)


def after(value, *events):
    return lax.optimization_barrier((value,) + events)[0]


def choose(flag, first, second):
    return jnp.where(flag, first, second)


def on_device(
    section_inputs,
    cotangent,
    conv_weight,
    out_weight,
    norm_scale,
    norm_shift,
    inner_scale,
    inner_shift,
):
    sections = lax.axis_size("section")
    windows = lax.axis_size("dp")
    count = lax.axis_size("seq")
    section = lax.axis_index("section")
    number = lax.axis_index("seq")
    window = lax.axis_index("dp")
    inputs = section_inputs[0, :, 0]
    top = cotangent[:, 0]
    micro, rows, channels = inputs.shape
    kernel = conv_weight[0]
    inner = kernel.shape[2]
    kernel_flat = kernel.reshape(3 * channels, inner)
    out_w = out_weight[0]
    own = BASE_DILATION // count
    step = (own * (1 + section % 2), own)
    gathered = count == 4 and windows == 2
    core, side = number % 2, number // 2
    ticks = micro + LAG * (sections - 1)

    def send_down(value, now):
        hops = [hop for hop in range(sections - 1) if 0 <= now - LAG * hop < micro]
        pairs = [(sections - 1 - hop, sections - 2 - hop) for hop in hops]
        return lax.ppermute(value, "section", pairs)

    def forward(block_in):
        pre = block_in.astype(jnp.float32) * norm_scale[0] + norm_shift[0]
        act, slope = gelu_pair(pre)
        hidden = act.astype(jnp.bfloat16)
        up, same, down = shifts(hidden, step)
        taps = jnp.concatenate([down, same, up], axis=-1)
        inner_pre = (
            jnp.dot(taps, kernel_flat, preferred_element_type=jnp.float32) * inner_scale[0]
            + inner_shift[0]
        )
        inner_act, inner_slope = gelu_pair(inner_pre)
        return lax.optimization_barrier(
            (
                hidden,
                slope * norm_scale[0],
                inner_act.astype(jnp.bfloat16),
                inner_slope * inner_scale[0],
            )
        )

    def transposed(unit):
        return lax.optimization_barrier(
            jnp.concatenate(
                [
                    lax.dot_general(
                        unit,
                        kernel[tap],
                        (((1,), (1,)), ((), ())),
                        preferred_element_type=jnp.float32,
                    ).astype(jnp.bfloat16)
                    for tap in range(3)
                ]
            )
        )

    if count == 4:

        def swap_sides(keep, come):
            send = jnp.stack([pick(keep, 1 - side, 1), pick(come, 1 - side, 1)], 1)
            mine = jnp.stack([pick(keep, side, 1), pick(come, side, 1)], 1)
            return send, mine

        def settle(mine, come):
            mine, come = (
                jnp.stack(
                    [
                        choose(core == 0, one[:, 0], one[:, 1]),
                        choose(core == 0, one[:, 1], one[:, 0]),
                    ],
                    1,
                )
                for one in (mine, come)
            )
            both = jnp.stack([choose(side == 0, mine, come), choose(side == 0, come, mine)], 1)
            both = both.reshape(-1, rows, channels)
            return both[0], both[1]

        send, keep = split_cores(section_inputs, cotangent, core, 0, 1)
        come = seq_swap(send, 1)
        later_core = after(core, send)
        later_send, later_keep = split_cores(section_inputs, cotangent, later_core, 1, micro - 1)
        later_come = seq_swap(later_send, 1)
        send, mine = swap_sides(keep, come)
        come = seq_swap(send, 2)
        later_keep = after(later_keep, send)
        later_send, later_mine = swap_sides(later_keep, later_come)
        parts = [later_send[2 * m : 2 * m + 2] for m in range(micro - 1)]
        parts = lax.optimization_barrier(tuple(parts) + (later_mine,))
        later_mine = parts[-1]
        back_kernel = transposed(after(jnp.eye(inner, dtype=jnp.bfloat16), *parts))
        come = after(come, *parts)
        arriving = [(mine, come)]

        def arrived(m, *events):
            mine, come = arriving[m]
            if m + 1 < micro:
                send = parts[m] if m == 0 else after(parts[m], *events)
                arriving.append((later_mine[2 * m : 2 * m + 2], seq_swap(send, 2)))
            return settle(mine, after(come, *events))
    else:
        swapped = to_residues(jnp.concatenate([inputs, top]), number)
        back_kernel = kernel.transpose(0, 2, 1).reshape(3 * inner, channels)

        def arrived(m, *events):
            return swapped[m], swapped[micro + m]

    tops, hidden, slope, inner_act, inner_slope = [], [], [], [], []

    def tick(index, received):
        def of_index(values):
            value = values[0]
            for m in range(1, len(values)):
                value = jnp.where(index >= m, values[m], value)
            return value

        grad_top = of_index(tops)
        if received is not None:
            grad_top = jnp.where(section == sections - 1, grad_top, received)
        grad_inner = lax.dot_general(
            grad_top, out_w, (((1,), (1,)), ((), ())), preferred_element_type=jnp.float32
        )
        grad_conv = (grad_inner * of_index(inner_slope)).astype(jnp.bfloat16)
        back = jnp.concatenate(shifts(grad_conv, step), axis=-1)
        grad_hidden = jnp.dot(back, back_kernel, preferred_element_type=jnp.float32)
        grad_block = (grad_top.astype(jnp.float32) + grad_hidden * of_index(slope)).astype(
            jnp.bfloat16
        )
        return lax.optimization_barrier((grad_top, grad_conv, grad_block))

    def of_section(m, which):
        value = done[m][which]
        for below in range(1, sections):
            value = jnp.where(
                section == sections - 1 - below, done[m + LAG * below][which], value
            )
        return value

    def exchange_rows(value, far_value):
        return jnp.concatenate(
            [choose(window == 0, value, far_value), choose(window == 0, far_value, value)]
        )

    half = channels // 2
    share = half // 2
    sent, done = [], []
    near_hidden, far_hidden = [], []
    near_grad, far_grad = [None] * micro, [None] * micro
    conv_total = 0.0
    out_part = 0.0
    for now in range(ticks):
        if now < micro:
            block_in, one_top = arrived(now, *([done[now - 1]] if now else []))
            one = forward(block_in)
            tops.append(one_top)
            hidden.append(one[0])
            slope.append(one[1])
            inner_act.append(one[2])
            inner_slope.append(one[3])
        received = None
        if now >= LAG:
            events = [done[now - 1]]
            if now < micro:
                events.append(hidden[now])
            if gathered and now == NEAR:
                events.append(near_hidden)
            if gathered and now == FAR:
                events.append(far_hidden)
            if gathered and now == ticks - 1:
                events.append(near_grad[0])
            received = after(sent[now - LAG], *events)
        done.append(tick(now - LAG * (sections - 1 - section), received))
        if now + LAG < ticks:
            sent.append(send_down(done[now][2], now))
        if gathered and now == micro - 1:
            wide = jnp.concatenate(after(tuple(hidden), done[now]))
            mine = choose(side == 0, wide[:, :half], wide[:, half:])
            other = choose(side == 0, wide[:, half:], wide[:, :half])
            near_hidden = (mine, seq_swap(other, 2))
        if gathered and now == micro:
            near_hidden = jnp.concatenate(
                [one.reshape(micro, rows, half) for one in after(near_hidden, done[now])], axis=1
            )
            far_hidden = dp_swap(near_hidden)
        m = now - LAG * (sections - 1)
        if m >= 0:
            out_part = out_part + lax.dot_general(
                of_section(m, 0),
                inner_act[m],
                (((0,), (0,)), ((), ())),
                preferred_element_type=jnp.float32,
            )
        if gathered and m >= 0:
            grad_conv = of_section(m, 1)
            near_grad[m] = (grad_conv, seq_swap(grad_conv, 2))
        if gathered and m >= 1:
            near_grad[m - 1] = jnp.concatenate(after(near_grad[m - 1], done[now]))
            far_grad[m - 1] = dp_swap(near_grad[m - 1])

    def add_conv(total, m, *events):
        if gathered:
            all_hidden = exchange_rows(near_hidden[m], far_hidden[m])
            all_grad = exchange_rows(near_grad[m], after(far_grad[m], *events))
            all_grad = all_grad.reshape(4, rows, inner)
            back = jnp.concatenate(shifts(all_grad, step), axis=-1).reshape(4 * rows, 3 * inner)
        else:
            all_hidden = hidden[m]
            back = jnp.concatenate(shifts(of_section(m, 1), step), axis=-1)
        return total + lax.dot_general(
            all_hidden, back, (((0,), (0,)), ((), ())), preferred_element_type=jnp.float32
        )

    if gathered:
        out_part = after(out_part, near_grad[1])
        quarters = out_part.reshape(2, 2, share, inner)
        keep = choose(core == 0, quarters[:, 0], quarters[:, 1])
        send = choose(core == 0, quarters[:, 1], quarters[:, 0]).astype(jnp.bfloat16)
        come_out = seq_swap(send, 1)
        far_grad[-2] = after(far_grad[-2], send, far_grad[0])
        near_grad[-1] = jnp.concatenate(after(near_grad[-1], far_grad[-2]))
        far_grad[-1] = dp_swap(near_grad[-1])
        come_out = after(come_out, near_grad[-1]).astype(jnp.float32)
        columns = [keep[0] + come_out[0], keep[1] + come_out[1]]
        send = choose(side == 0, columns[1], columns[0]).astype(jnp.bfloat16)
        keep = choose(side == 0, columns[0], columns[1])
        come = seq_swap(send, 2)
        grads = jnp.stack([of_section(m, 2) for m in range(micro)])
        grads_out, arrived_last = from_residues(after(grads, send), number)
        for m in range(micro - 1):
            conv_total = lax.optimization_barrier(add_conv(conv_total, m, send))
        come = after(come, conv_total)
        columns = (keep + come.astype(jnp.float32)).astype(jnp.bfloat16)
        come_out = dp_swap(columns)
        conv_total = add_conv(conv_total, micro - 1, columns, arrived_last)
        out_sum = (columns.astype(jnp.float32) + come_out.astype(jnp.float32)).T
    else:
        for m in range(micro):
            conv_total = add_conv(conv_total, m)
        grads_out, _ = from_residues(jnp.stack([of_section(m, 2) for m in range(micro)]), number)

    factor = 1.0 / float(micro * windows)
    if gathered:
        low, high = conv_total[:share], conv_total[share:]
        come = seq_swap(choose(core == 0, high, low).astype(jnp.bfloat16), 1)
        conv_sum = choose(core == 0, low, high) + come.astype(jnp.float32)
        conv_sum = jnp.stack([conv_sum[:, k * inner : (k + 1) * inner] for k in range(3)])
    else:
        out_part = out_part.T
        conv_part = conv_total.reshape(channels, 3, inner).transpose(1, 0, 2)
        conv_sum, out_sum = (
            lax.psum(
                lax.psum_scatter(part.astype(jnp.bfloat16), "seq", scatter_dimension=1, tiled=True),
                "dp",
            ).astype(jnp.float32)
            for part in (conv_part, out_part)
        )
    return (
        grads_out.reshape(section_inputs.shape),
        (conv_sum * factor)[None],
        (out_sum * factor)[None],
    )


def solution(mesh):
    return jax.shard_map(
        on_device,
        mesh=mesh,
        in_specs=(
            P("section", None, "dp", "seq", None),
            P(None, "dp", "seq", None),
            P("section", None, None, None),
            P("section", None, None),
            P("section", None),
            P("section", None),
            P("section", None),
            P("section", None),
        ),
        out_specs=(
            P("section", None, "dp", "seq", None),
            P("section", None, "seq", None),
            P("section", None, "seq"),
        ),
        check_vma=False,
    )
```

```python
import jax
import jax.numpy as jnp
from jax import lax
from jax.experimental import pallas as pl
from jax.experimental.pallas import tpu as pltpu
from jax.sharding import PartitionSpec as P

BASE_DILATION = 32
LAG = 2
NEAR = 5
FAR = 8


gelu_coeff = 0.7978845608028654
cubic_coeff = 0.044715


def gelu_pair(inputs):
    squared = inputs * inputs
    inner_arg = gelu_coeff * (inputs + cubic_coeff * inputs * squared)
    tanh_val = jnp.tanh(inner_arg)
    result = 0.5 * inputs * (1.0 + tanh_val)
    slope_val = 0.5 * (1.0 + tanh_val) + 0.5 * inputs * (1.0 - tanh_val * tanh_val) * gelu_coeff * (
        1.0 + 3.0 * cubic_coeff * squared
    )
    return (result, slope_val)


def seq_swap(value, bit):
    count = lax.axis_size("seq")
    return lax.ppermute(value, "seq", [(i, i ^ bit) for i in range(count)])


def dp_swap(value):
    return lax.ppermute(value, "dp", [(0, 1), (1, 0)])


def pick(value, index, axis):
    return lax.dynamic_index_in_dim(value, index, axis, keepdims=False)


def exchange(value, number):
    count = lax.axis_size("seq")
    bit = 1
    comes = []
    while bit < count:
        batch, source, inner, target, rest, channels = value.shape
        split = value.reshape(batch, source, inner, target // 2, 2, rest, channels)
        mine = (number // bit) % 2
        keep = pick(split, mine, 4)
        come = seq_swap(pick(split, 1 - mine, 4), bit)
        comes.append(come)
        first = jnp.where(mine == 0, keep, come)
        second = jnp.where(mine == 0, come, keep)
        value = jnp.stack([first, second], axis=1).reshape(
            batch, 2 * source, inner, target // 2, rest, channels
        )
        bit *= 2
    return value[:, :, :, 0], comes


def to_residues(value, number):
    batch, rows, channels = value.shape
    count = lax.axis_size("seq")
    value = value.reshape(batch, 1, rows // BASE_DILATION, count, BASE_DILATION // count, channels)
    return exchange(value, number)[0].reshape(batch, rows, channels)


def from_residues(value, number):
    batch, rows, channels = value.shape
    count = lax.axis_size("seq")
    own = BASE_DILATION // count
    inner = rows // BASE_DILATION
    value = value.reshape(batch, 1, count, inner, own, channels).transpose(0, 1, 3, 2, 4, 5)
    value, comes = exchange(value, number)
    return value.transpose(0, 2, 1, 3, 4).reshape(batch, rows, channels), comes


def shifts(value, step):
    rows = value.shape[-2]
    width = 2 * step[1]
    pad = [(0, 0)] * (value.ndim - 2) + [(width, width), (0, 0)]
    padded = jnp.pad(value, pad)
    axis = value.ndim - 2
    return [
        lax.dynamic_slice_in_dim(padded, width - (tap - 1) * step[0], rows, axis) for tap in range(3)
    ]


def split_cores(section_inputs, cotangent, core, first, batch):
    rows, channels = cotangent.shape[2:]
    quarter = rows // 4
    blocks = rows // BASE_DILATION

    def kernel(core_ref, inputs_ref, top_ref, send_ref, keep_ref):
        low = core_ref[0] == 0
        for which, value in enumerate((inputs_ref[0, 0, 0], top_ref[0, 0])):
            value = value.astype(jnp.float32).reshape(blocks, 4, quarter // blocks, channels)
            for side in range(2):
                first_part = value[:, 2 * side].reshape(quarter, channels)
                second_part = value[:, 2 * side + 1].reshape(quarter, channels)
                keep = jnp.where(low, first_part, second_part)
                send = jnp.where(low, second_part, first_part)
                keep_ref[which, side] = keep.astype(keep_ref.dtype)
                send_ref[which, side] = send.astype(send_ref.dtype)

    out = jax.ShapeDtypeStruct((2 * batch, 2, quarter, channels), cotangent.dtype)
    part = pl.BlockSpec((2, 2, quarter, channels), lambda m: (m, 0, 0, 0))
    return pl.pallas_call(
        kernel,
        grid=(batch,),
        in_specs=[
            pl.BlockSpec(memory_space=pltpu.SMEM),
            pl.BlockSpec((1, 1, 1, rows, channels), lambda m: (0, first + m, 0, 0, 0)),
            pl.BlockSpec((1, 1, rows, channels), lambda m: (first + m, 0, 0, 0)),
        ],
        out_specs=[part, part],
        out_shape=[out, out],
        compiler_params=pltpu.CompilerParams(vmem_limit_bytes=16 * 2**20),
        cost_estimate=pl.CostEstimate(
            flops=0, bytes_accessed=8 * batch * rows * channels, transcendentals=0
        ),
    )(core.reshape(1).astype(jnp.int32), section_inputs, cotangent)


def after(value, *events):
    return lax.optimization_barrier((value,) + events)[0]


def choose(flag, first, second):
    return jnp.where(flag, first, second)


def on_device(
    section_inputs,
    cotangent,
    conv_weight,
    out_weight,
    norm_scale,
    norm_shift,
    inner_scale,
    inner_shift,
):
    sections = lax.axis_size("section")
    windows = lax.axis_size("dp")
    count = lax.axis_size("seq")
    section = lax.axis_index("section")
    number = lax.axis_index("seq")
    window = lax.axis_index("dp")
    inputs = section_inputs[0, :, 0]
    top = cotangent[:, 0]
    micro, rows, channels = inputs.shape
    kernel = conv_weight[0]
    inner = kernel.shape[2]
    kernel_flat = kernel.reshape(3 * channels, inner)
    out_w = out_weight[0]
    own = BASE_DILATION // count
    step = (own * (1 + section % 2), own)
    gathered = count == 4 and windows == 2
    core, side = number % 2, number // 2
    ticks = micro + LAG * (sections - 1)

    def send_down(value, now):
        hops = [hop for hop in range(sections - 1) if 0 <= now - LAG * hop < micro]
        return {
            hop: lax.ppermute(value, "section", [(sections - 1 - hop, sections - 2 - hop)])
            for hop in reversed(hops)
        }

    def receive(comes, *events):
        value = None
        for hop, come in comes.items():
            come = after(come, *events)
            events = (come,)
            value = come if value is None else jnp.where(section == sections - 2 - hop, come, value)
        return value

    def forward(block_in):
        pre = block_in.astype(jnp.float32) * norm_scale[0] + norm_shift[0]
        act, slope = gelu_pair(pre)
        hidden = act.astype(jnp.bfloat16)
        up, same, down = shifts(hidden, step)
        taps = jnp.concatenate([down, same, up], axis=-1)
        inner_pre = (
            jnp.dot(taps, kernel_flat, preferred_element_type=jnp.float32) * inner_scale[0]
            + inner_shift[0]
        )
        inner_act, inner_slope = gelu_pair(inner_pre)
        return lax.optimization_barrier(
            (
                hidden,
                slope * norm_scale[0],
                inner_act.astype(jnp.bfloat16),
                inner_slope * inner_scale[0],
            )
        )

    def transposed(unit):
        return lax.optimization_barrier(
            jnp.concatenate(
                [
                    lax.dot_general(
                        unit,
                        kernel[tap],
                        (((1,), (1,)), ((), ())),
                        preferred_element_type=jnp.float32,
                    ).astype(jnp.bfloat16)
                    for tap in range(3)
                ]
            )
        )

    if count == 4:

        def swap_sides(keep, come):
            send = jnp.stack([pick(keep, 1 - side, 1), pick(come, 1 - side, 1)], 1)
            mine = jnp.stack([pick(keep, side, 1), pick(come, side, 1)], 1)
            return send, mine

        def settle(mine, come):
            mine, come = (
                jnp.stack(
                    [
                        choose(core == 0, one[:, 0], one[:, 1]),
                        choose(core == 0, one[:, 1], one[:, 0]),
                    ],
                    1,
                )
                for one in (mine, come)
            )
            both = jnp.stack([choose(side == 0, mine, come), choose(side == 0, come, mine)], 1)
            both = both.reshape(-1, rows, channels)
            return both[0], both[1]

        send, keep = split_cores(section_inputs, cotangent, core, 0, 1)
        come = seq_swap(send, 1)
        later_core = after(core, send)
        later_send, later_keep = split_cores(section_inputs, cotangent, later_core, 1, micro - 1)
        later_come = seq_swap(later_send, 1)
        send, mine = swap_sides(keep, come)
        come = seq_swap(send, 2)
        later_keep = after(later_keep, send)
        later_send, later_mine = swap_sides(later_keep, later_come)
        parts = [later_send[2 * m : 2 * m + 2] for m in range(micro - 1)]
        parts = lax.optimization_barrier(tuple(parts) + (later_mine,))
        later_mine = parts[-1]
        back_kernel = transposed(after(jnp.eye(inner, dtype=jnp.bfloat16), *parts))
        come = after(come, *parts)
        arriving = [(mine, come)]

        def arrived(m, *events):
            mine, come = arriving[m]
            if m + 1 < micro:
                send = parts[m] if m == 0 else after(parts[m], *events)
                arriving.append((later_mine[2 * m : 2 * m + 2], seq_swap(send, 2)))
            return settle(mine, after(come, *events))
    else:
        swapped = to_residues(jnp.concatenate([inputs, top]), number)
        back_kernel = kernel.transpose(0, 2, 1).reshape(3 * inner, channels)

        def arrived(m, *events):
            return swapped[m], swapped[micro + m]

    tops, hidden, slope, inner_act, inner_slope = [], [], [], [], []

    def tick(index, received):
        def of_index(values):
            value = values[0]
            for m in range(1, len(values)):
                value = jnp.where(index >= m, values[m], value)
            return value

        grad_top = of_index(tops)
        if received is not None:
            grad_top = jnp.where(section == sections - 1, grad_top, received)
        grad_inner = lax.dot_general(
            grad_top, out_w, (((1,), (1,)), ((), ())), preferred_element_type=jnp.float32
        )
        grad_conv = (grad_inner * of_index(inner_slope)).astype(jnp.bfloat16)
        back = jnp.concatenate(shifts(grad_conv, step), axis=-1)
        grad_hidden = jnp.dot(back, back_kernel, preferred_element_type=jnp.float32)
        grad_block = (grad_top.astype(jnp.float32) + grad_hidden * of_index(slope)).astype(
            jnp.bfloat16
        )
        return lax.optimization_barrier((grad_top, grad_conv, grad_block))

    def of_section(m, which):
        value = done[m][which]
        for below in range(1, sections):
            value = jnp.where(
                section == sections - 1 - below, done[m + LAG * below][which], value
            )
        return value

    def exchange_rows(value, far_value):
        return jnp.concatenate(
            [choose(window == 0, value, far_value), choose(window == 0, far_value, value)]
        )

    half = channels // 2
    share = half // 2
    sent, done = [], []
    near_hidden, far_hidden = [], []
    near_grad, far_grad = [None] * micro, [None] * micro
    conv_total = 0.0
    out_part = 0.0
    for now in range(ticks):
        if now < micro:
            block_in, one_top = arrived(now, *([done[now - 1]] if now else []))
            one = forward(block_in)
            tops.append(one_top)
            hidden.append(one[0])
            slope.append(one[1])
            inner_act.append(one[2])
            inner_slope.append(one[3])
        received = None
        if now >= LAG:
            events = [done[now - 1]]
            if now < micro:
                events.append(hidden[now])
            if gathered and now == NEAR:
                events.append(near_hidden)
            if gathered and now == FAR:
                events.append(far_hidden)
            if gathered and now == ticks - 1:
                events += [near_grad[0], comes_early[0]]
            received = receive(sent[now - LAG], *events)
        done.append(tick(now - LAG * (sections - 1 - section), received))
        if now + LAG < ticks:
            sent.append(send_down(done[now][2], now))
        if gathered and now == micro - 1:
            wide = jnp.concatenate(after(tuple(hidden), done[now]))
            mine = choose(side == 0, wide[:, :half], wide[:, half:])
            other = choose(side == 0, wide[:, half:], wide[:, :half])
            near_hidden = (mine, seq_swap(other, 2))
        if gathered and now == micro:
            near_hidden = jnp.concatenate(
                [one.reshape(micro, rows, half) for one in after(near_hidden, done[now])], axis=1
            )
            far_hidden = dp_swap(near_hidden)
        m = now - LAG * (sections - 1)
        if m >= 0:
            out_part = out_part + lax.dot_general(
                of_section(m, 0),
                inner_act[m],
                (((0,), (0,)), ((), ())),
                preferred_element_type=jnp.float32,
            )
        if gathered and m >= 0:
            grad_conv = of_section(m, 1)
            near_grad[m] = (grad_conv, seq_swap(grad_conv, 2))
        if gathered and m >= 1:
            near_grad[m - 1] = jnp.concatenate(after(near_grad[m - 1], done[now]))
            far_grad[m - 1] = dp_swap(near_grad[m - 1])
        if gathered and m == micro - 2:
            early = jnp.stack([of_section(one, 2) for one in range(micro - 1)])
            early, comes_early = from_residues(early, number)

    def add_conv(total, m, *events):
        if gathered:
            all_hidden = exchange_rows(near_hidden[m], far_hidden[m])
            all_grad = exchange_rows(near_grad[m], after(far_grad[m], *events))
            all_grad = all_grad.reshape(4, rows, inner)
            back = jnp.concatenate(shifts(all_grad, step), axis=-1).reshape(4 * rows, 3 * inner)
        else:
            all_hidden = hidden[m]
            back = jnp.concatenate(shifts(of_section(m, 1), step), axis=-1)
        return total + lax.dot_general(
            all_hidden, back, (((0,), (0,)), ((), ())), preferred_element_type=jnp.float32
        )

    if gathered:
        out_part = after(out_part, near_grad[1])
        quarters = out_part.reshape(2, 2, share, inner)
        keep = choose(core == 0, quarters[:, 0], quarters[:, 1])
        send = choose(core == 0, quarters[:, 1], quarters[:, 0]).astype(jnp.bfloat16)
        come_out = seq_swap(send, 1)
        near_grad[-1] = jnp.concatenate(after(near_grad[-1], send))
        far_grad[-1] = dp_swap(near_grad[-1])
        far_grad[-2] = after(far_grad[-2], near_grad[-1])
        come_out = after(come_out, near_grad[-1]).astype(jnp.float32)
        columns = [keep[0] + come_out[0], keep[1] + come_out[1]]
        send = choose(side == 0, columns[1], columns[0]).astype(jnp.bfloat16)
        keep = choose(side == 0, columns[0], columns[1])
        come = seq_swap(send, 2)
        late = after(of_section(micro - 1, 2)[None], send)
        late, comes_late = from_residues(late, number)
        grads_out = jnp.concatenate([early, late])
        for m in range(micro - 1):
            events = [send] if m == 0 else [send, comes_early[-1]]
            conv_total = lax.optimization_barrier(add_conv(conv_total, m, *events))
        come = after(come, conv_total)
        columns = (keep + come.astype(jnp.float32)).astype(jnp.bfloat16)
        come_out = dp_swap(columns)
        conv_total = add_conv(conv_total, micro - 1, columns)
        out_sum = (columns.astype(jnp.float32) + come_out.astype(jnp.float32)).T
    else:
        for m in range(micro):
            conv_total = add_conv(conv_total, m)
        grads_out, _ = from_residues(jnp.stack([of_section(m, 2) for m in range(micro)]), number)

    factor = 1.0 / float(micro * windows)
    if gathered:
        low, high = conv_total[:share], conv_total[share:]
        come = seq_swap(choose(core == 0, high, low).astype(jnp.bfloat16), 1)
        come = after(come, comes_late[-1])
        conv_sum = choose(core == 0, low, high) + come.astype(jnp.float32)
        conv_sum = jnp.stack([conv_sum[:, k * inner : (k + 1) * inner] for k in range(3)])
    else:
        out_part = out_part.T
        conv_part = conv_total.reshape(channels, 3, inner).transpose(1, 0, 2)
        conv_sum, out_sum = (
            lax.psum(
                lax.psum_scatter(part.astype(jnp.bfloat16), "seq", scatter_dimension=1, tiled=True),
                "dp",
            ).astype(jnp.float32)
            for part in (conv_part, out_part)
        )
    return (
        grads_out.reshape(section_inputs.shape),
        (conv_sum * factor)[None],
        (out_sum * factor)[None],
    )


def solution(mesh):
    return jax.shard_map(
        on_device,
        mesh=mesh,
        in_specs=(
            P("section", None, "dp", "seq", None),
            P(None, "dp", "seq", None),
            P("section", None, None, None),
            P("section", None, None),
            P("section", None),
            P("section", None),
            P("section", None),
            P("section", None),
        ),
        out_specs=(
            P("section", None, "dp", "seq", None),
            P("section", None, "seq", None),
            P("section", None, "seq"),
        ),
        check_vma=False,
    )
```

```python
import jax
import jax.numpy as jnp
from jax import lax
from jax.experimental import pallas as pl
from jax.experimental.pallas import tpu as pltpu
from jax.sharding import PartitionSpec as P

BASE_DILATION = 32
LAG = 2
NEAR = 5
FAR = 8


gelu_coeff = 0.7978845608028654
cubic_coeff = 0.044715


def gelu_pair(inputs):
    squared = inputs * inputs
    inner_arg = gelu_coeff * (inputs + cubic_coeff * inputs * squared)
    tanh_val = jnp.tanh(inner_arg)
    result = 0.5 * inputs * (1.0 + tanh_val)
    slope_val = 0.5 * (1.0 + tanh_val) + 0.5 * inputs * (1.0 - tanh_val * tanh_val) * gelu_coeff * (
        1.0 + 3.0 * cubic_coeff * squared
    )
    return (result, slope_val)


def seq_swap(value, bit):
    count = lax.axis_size("seq")
    return lax.ppermute(value, "seq", [(i, i ^ bit) for i in range(count)])


def dp_swap(value):
    return lax.ppermute(value, "dp", [(0, 1), (1, 0)])


def pick(value, index, axis):
    return lax.dynamic_index_in_dim(value, index, axis, keepdims=False)


def exchange(value, number):
    count = lax.axis_size("seq")
    bit = 1
    comes = []
    while bit < count:
        batch, source, inner, target, rest, channels = value.shape
        split = value.reshape(batch, source, inner, target // 2, 2, rest, channels)
        mine = (number // bit) % 2
        keep = pick(split, mine, 4)
        come = seq_swap(pick(split, 1 - mine, 4), bit)
        comes.append(come)
        first = jnp.where(mine == 0, keep, come)
        second = jnp.where(mine == 0, come, keep)
        value = jnp.stack([first, second], axis=1).reshape(
            batch, 2 * source, inner, target // 2, rest, channels
        )
        bit *= 2
    return value[:, :, :, 0], comes


def to_residues(value, number):
    batch, rows, channels = value.shape
    count = lax.axis_size("seq")
    value = value.reshape(batch, 1, rows // BASE_DILATION, count, BASE_DILATION // count, channels)
    return exchange(value, number)[0].reshape(batch, rows, channels)


def from_residues(value, number):
    batch, rows, channels = value.shape
    count = lax.axis_size("seq")
    own = BASE_DILATION // count
    inner = rows // BASE_DILATION
    value = value.reshape(batch, 1, count, inner, own, channels).transpose(0, 1, 3, 2, 4, 5)
    value, comes = exchange(value, number)
    return value.transpose(0, 2, 1, 3, 4).reshape(batch, rows, channels), comes


def shifts(value, step):
    rows = value.shape[-2]
    width = 2 * step[1]
    pad = [(0, 0)] * (value.ndim - 2) + [(width, width), (0, 0)]
    padded = jnp.pad(value, pad)
    axis = value.ndim - 2
    return [
        lax.dynamic_slice_in_dim(padded, width - (tap - 1) * step[0], rows, axis) for tap in range(3)
    ]


def split_cores(section_inputs, cotangent, core, first, batch):
    rows, channels = cotangent.shape[2:]
    quarter = rows // 4
    blocks = rows // BASE_DILATION

    def kernel(core_ref, inputs_ref, top_ref, send_ref, keep_ref):
        low = core_ref[0] == 0
        for which, value in enumerate((inputs_ref[0, 0, 0], top_ref[0, 0])):
            value = value.astype(jnp.float32).reshape(blocks, 4, quarter // blocks, channels)
            for side in range(2):
                first_part = value[:, 2 * side].reshape(quarter, channels)
                second_part = value[:, 2 * side + 1].reshape(quarter, channels)
                keep = jnp.where(low, first_part, second_part)
                send = jnp.where(low, second_part, first_part)
                keep_ref[which, side] = keep.astype(keep_ref.dtype)
                send_ref[which, side] = send.astype(send_ref.dtype)

    out = jax.ShapeDtypeStruct((2 * batch, 2, quarter, channels), cotangent.dtype)
    part = pl.BlockSpec((2, 2, quarter, channels), lambda m: (m, 0, 0, 0))
    return pl.pallas_call(
        kernel,
        grid=(batch,),
        in_specs=[
            pl.BlockSpec(memory_space=pltpu.SMEM),
            pl.BlockSpec((1, 1, 1, rows, channels), lambda m: (0, first + m, 0, 0, 0)),
            pl.BlockSpec((1, 1, rows, channels), lambda m: (first + m, 0, 0, 0)),
        ],
        out_specs=[part, part],
        out_shape=[out, out],
        compiler_params=pltpu.CompilerParams(vmem_limit_bytes=16 * 2**20),
        cost_estimate=pl.CostEstimate(
            flops=0, bytes_accessed=8 * batch * rows * channels, transcendentals=0
        ),
    )(core.reshape(1).astype(jnp.int32), section_inputs, cotangent)


def after(value, *events):
    return lax.optimization_barrier((value,) + events)[0]


def choose(flag, first, second):
    return jnp.where(flag, first, second)


def on_device(
    section_inputs,
    cotangent,
    conv_weight,
    out_weight,
    norm_scale,
    norm_shift,
    inner_scale,
    inner_shift,
):
    sections = lax.axis_size("section")
    windows = lax.axis_size("dp")
    count = lax.axis_size("seq")
    section = lax.axis_index("section")
    number = lax.axis_index("seq")
    window = lax.axis_index("dp")
    inputs = section_inputs[0, :, 0]
    top = cotangent[:, 0]
    micro, rows, channels = inputs.shape
    kernel = conv_weight[0]
    inner = kernel.shape[2]
    kernel_flat = kernel.reshape(3 * channels, inner)
    out_w = out_weight[0]
    own = BASE_DILATION // count
    step = (own * (1 + section % 2), own)
    gathered = count == 4 and windows == 2
    core, side = number % 2, number // 2
    ticks = micro + LAG * (sections - 1)

    def send_down(value, now):
        hops = [hop for hop in range(sections - 1) if 0 <= now - LAG * hop < micro]
        return {
            hop: lax.ppermute(value, "section", [(sections - 1 - hop, sections - 2 - hop)])
            for hop in reversed(hops)
        }

    def receive(comes, *events):
        value = None
        for hop, come in comes.items():
            come = after(come, *events)
            events = (come,)
            value = come if value is None else jnp.where(section == sections - 2 - hop, come, value)
        return value

    def forward(block_in):
        pre = block_in.astype(jnp.float32) * norm_scale[0] + norm_shift[0]
        act, slope = gelu_pair(pre)
        hidden = act.astype(jnp.bfloat16)
        up, same, down = shifts(hidden, step)
        taps = jnp.concatenate([down, same, up], axis=-1)
        inner_pre = (
            jnp.dot(taps, kernel_flat, preferred_element_type=jnp.float32) * inner_scale[0]
            + inner_shift[0]
        )
        inner_act, inner_slope = gelu_pair(inner_pre)
        return lax.optimization_barrier(
            (
                hidden,
                slope * norm_scale[0],
                inner_act.astype(jnp.bfloat16),
                inner_slope * inner_scale[0],
            )
        )

    def transposed(unit):
        return lax.optimization_barrier(
            jnp.concatenate(
                [
                    lax.dot_general(
                        unit,
                        kernel[tap],
                        (((1,), (1,)), ((), ())),
                        preferred_element_type=jnp.float32,
                    ).astype(jnp.bfloat16)
                    for tap in range(3)
                ]
            )
        )

    if count == 4:

        def swap_sides(keep, come):
            send = jnp.stack([pick(keep, 1 - side, 1), pick(come, 1 - side, 1)], 1)
            mine = jnp.stack([pick(keep, side, 1), pick(come, side, 1)], 1)
            return send, mine

        def settle(mine, come):
            mine, come = (
                jnp.stack(
                    [
                        choose(core == 0, one[:, 0], one[:, 1]),
                        choose(core == 0, one[:, 1], one[:, 0]),
                    ],
                    1,
                )
                for one in (mine, come)
            )
            both = jnp.stack([choose(side == 0, mine, come), choose(side == 0, come, mine)], 1)
            both = both.reshape(-1, rows, channels)
            return both[0], both[1]

        send, keep = split_cores(section_inputs, cotangent, core, 0, 1)
        come = seq_swap(send, 1)
        later_core = after(core, send)
        later_send, later_keep = split_cores(section_inputs, cotangent, later_core, 1, micro - 1)
        later_come = seq_swap(later_send, 1)
        send, mine = swap_sides(keep, come)
        come = seq_swap(send, 2)
        later_keep = after(later_keep, send)
        later_send, later_mine = swap_sides(later_keep, later_come)
        parts = [later_send[2 * m : 2 * m + 2] for m in range(micro - 1)]
        parts = lax.optimization_barrier(tuple(parts) + (later_mine,))
        later_mine = parts[-1]
        back_kernel = transposed(after(jnp.eye(inner, dtype=jnp.bfloat16), *parts))
        come = after(come, *parts)
        arriving = [(mine, come)]

        def arrived(m, *events):
            mine, come = arriving[m]
            if m + 1 < micro:
                send = parts[m] if m == 0 else after(parts[m], *events)
                arriving.append((later_mine[2 * m : 2 * m + 2], seq_swap(send, 2)))
            return settle(mine, after(come, *events))
    else:
        swapped = to_residues(jnp.concatenate([inputs, top]), number)
        back_kernel = kernel.transpose(0, 2, 1).reshape(3 * inner, channels)

        def arrived(m, *events):
            return swapped[m], swapped[micro + m]

    tops, hidden, slope, inner_act, inner_slope = [], [], [], [], []

    def tick(index, received):
        def of_index(values):
            value = values[0]
            for m in range(1, len(values)):
                value = jnp.where(index >= m, values[m], value)
            return value

        grad_top = of_index(tops)
        if received is not None:
            grad_top = jnp.where(section == sections - 1, grad_top, received)
        grad_inner = lax.dot_general(
            grad_top, out_w, (((1,), (1,)), ((), ())), preferred_element_type=jnp.float32
        )
        grad_conv = (grad_inner * of_index(inner_slope)).astype(jnp.bfloat16)
        back = jnp.concatenate(shifts(grad_conv, step), axis=-1)
        grad_hidden = jnp.dot(back, back_kernel, preferred_element_type=jnp.float32)
        grad_block = (grad_top.astype(jnp.float32) + grad_hidden * of_index(slope)).astype(
            jnp.bfloat16
        )
        return lax.optimization_barrier((grad_top, grad_conv, grad_block))

    def of_section(m, which):
        value = done[m][which]
        for below in range(1, sections):
            value = jnp.where(
                section == sections - 1 - below, done[m + LAG * below][which], value
            )
        return value

    def exchange_rows(value, far_value):
        return jnp.concatenate(
            [choose(window == 0, value, far_value), choose(window == 0, far_value, value)]
        )

    half = channels // 2
    share = half // 2
    sent, done = [], []
    near_hidden, far_hidden = [], []
    near_grad, far_grad = [None] * micro, [None] * micro
    conv_total = 0.0
    out_part = 0.0
    for now in range(ticks):
        if now < micro:
            block_in, one_top = arrived(now, *([done[now - 1]] if now else []))
            one = forward(block_in)
            tops.append(one_top)
            hidden.append(one[0])
            slope.append(one[1])
            inner_act.append(one[2])
            inner_slope.append(one[3])
        received = None
        if now >= LAG:
            events = [done[now - 1]]
            if now < micro:
                events.append(hidden[now])
            if gathered and now == NEAR:
                events.append(near_hidden)
            if gathered and now == FAR:
                events.append(far_hidden)
            if gathered and now == ticks - 1:
                events += [near_grad[0], comes_early[0]]
            received = receive(sent[now - LAG], *events)
        done.append(tick(now - LAG * (sections - 1 - section), received))
        if now + LAG < ticks:
            sent.append(send_down(done[now][2], now))
        if gathered and now == micro - 1:
            wide = jnp.concatenate(after(tuple(hidden), done[now]))
            mine = choose(side == 0, wide[:, :half], wide[:, half:])
            other = choose(side == 0, wide[:, half:], wide[:, :half])
            near_hidden = (mine, seq_swap(other, 2))
        if gathered and now == micro:
            near_hidden = jnp.concatenate(
                [one.reshape(micro, rows, half) for one in after(near_hidden, done[now])], axis=1
            )
            far_hidden = dp_swap(near_hidden)
        m = now - LAG * (sections - 1)
        if m >= 0:
            out_part = out_part + lax.dot_general(
                of_section(m, 0),
                inner_act[m],
                (((0,), (0,)), ((), ())),
                preferred_element_type=jnp.float32,
            )
        if gathered and m >= 0:
            grad_conv = of_section(m, 1)
            near_grad[m] = (grad_conv, seq_swap(grad_conv, 2))
        if gathered and m >= 1:
            near_grad[m - 1] = jnp.concatenate(after(near_grad[m - 1], done[now]))
            far_grad[m - 1] = dp_swap(near_grad[m - 1])
        if gathered and m == micro - 2:
            early = jnp.stack([of_section(one, 2) for one in range(micro - 1)])
            early, comes_early = from_residues(early, number)

    def add_conv(total, m, *events):
        if gathered:
            all_hidden = exchange_rows(near_hidden[m], far_hidden[m])
            all_grad = exchange_rows(near_grad[m], after(far_grad[m], *events))
            all_grad = all_grad.reshape(4, rows, inner)
            back = jnp.concatenate(shifts(all_grad, step), axis=-1).reshape(4 * rows, 3 * inner)
        else:
            all_hidden = hidden[m]
            back = jnp.concatenate(shifts(of_section(m, 1), step), axis=-1)
        return total + lax.dot_general(
            all_hidden, back, (((0,), (0,)), ((), ())), preferred_element_type=jnp.float32
        )

    if gathered:
        out_part = after(out_part, near_grad[1])
        quarters = out_part.reshape(2, 2, share, inner)
        keep = choose(core == 0, quarters[:, 0], quarters[:, 1])
        send = choose(core == 0, quarters[:, 1], quarters[:, 0]).astype(jnp.bfloat16)
        come_out = seq_swap(send, 1)
        come_out = after(come_out, near_grad[1]).astype(jnp.float32)
        columns = [keep[0] + come_out[0], keep[1] + come_out[1]]
        send = choose(side == 0, columns[1], columns[0]).astype(jnp.bfloat16)
        keep = choose(side == 0, columns[0], columns[1])
        come = seq_swap(send, 2)
        near_grad[-1] = jnp.concatenate(after(near_grad[-1], send))
        far_grad[-1] = dp_swap(near_grad[-1])
        far_grad[-2] = after(far_grad[-2], near_grad[-1])
        late = after(of_section(micro - 1, 2)[None], send)
        late, comes_late = from_residues(late, number)
        grads_out = jnp.concatenate([early, late])
        for m in range(micro - 1):
            events = [send] if m == 0 else [send, comes_early[-1]]
            conv_total = lax.optimization_barrier(add_conv(conv_total, m, *events))
        come = after(come, conv_total)
        columns = (keep + come.astype(jnp.float32)).astype(jnp.bfloat16)
        come_out = dp_swap(columns)
        conv_total = add_conv(conv_total, micro - 1, columns)
    else:
        for m in range(micro):
            conv_total = add_conv(conv_total, m)
        grads_out, _ = from_residues(jnp.stack([of_section(m, 2) for m in range(micro)]), number)

    factor = 1.0 / float(micro * windows)
    if gathered:
        low, high = conv_total[:share], conv_total[share:]
        come = seq_swap(choose(core == 0, high, low).astype(jnp.bfloat16), 1)
        come = after(come, comes_late[-1])
        conv_sum = choose(core == 0, low, high) + come.astype(jnp.float32)
        conv_sum = jnp.stack([conv_sum[:, k * inner : (k + 1) * inner] for k in range(3)])
        conv_sum = conv_sum * factor
        come_out = after(come_out, conv_sum)
        out_sum = (columns.astype(jnp.float32) + come_out.astype(jnp.float32)).T
    else:
        out_part = out_part.T
        conv_part = conv_total.reshape(channels, 3, inner).transpose(1, 0, 2)
        conv_sum, out_sum = (
            lax.psum(
                lax.psum_scatter(part.astype(jnp.bfloat16), "seq", scatter_dimension=1, tiled=True),
                "dp",
            ).astype(jnp.float32)
            for part in (conv_part, out_part)
        )
        conv_sum = conv_sum * factor
    return (
        grads_out.reshape(section_inputs.shape),
        conv_sum[None],
        (out_sum * factor)[None],
    )


def solution(mesh):
    return jax.shard_map(
        on_device,
        mesh=mesh,
        in_specs=(
            P("section", None, "dp", "seq", None),
            P(None, "dp", "seq", None),
            P("section", None, None, None),
            P("section", None, None),
            P("section", None),
            P("section", None),
            P("section", None),
            P("section", None),
        ),
        out_specs=(
            P("section", None, "dp", "seq", None),
            P("section", None, "seq", None),
            P("section", None, "seq"),
        ),
        check_vma=False,
    )
```

```python
import jax
import jax.numpy as jnp
from jax import lax
from jax.experimental import pallas as pl
from jax.experimental.pallas import tpu as pltpu
from jax.sharding import PartitionSpec as P

BASE_DILATION = 32
LAG = 2
NEAR = 5
FAR = 8


gelu_coeff = 0.7978845608028654
cubic_coeff = 0.044715


def gelu_pair(inputs):
    squared = inputs * inputs
    inner_arg = gelu_coeff * (inputs + cubic_coeff * inputs * squared)
    tanh_val = jnp.tanh(inner_arg)
    result = 0.5 * inputs * (1.0 + tanh_val)
    slope_val = 0.5 * (1.0 + tanh_val) + 0.5 * inputs * (1.0 - tanh_val * tanh_val) * gelu_coeff * (
        1.0 + 3.0 * cubic_coeff * squared
    )
    return (result, slope_val)


def seq_swap(value, bit):
    count = lax.axis_size("seq")
    return lax.ppermute(value, "seq", [(i, i ^ bit) for i in range(count)])


def dp_swap(value):
    return lax.ppermute(value, "dp", [(0, 1), (1, 0)])


def pick(value, index, axis):
    return lax.dynamic_index_in_dim(value, index, axis, keepdims=False)


def exchange(value, number):
    count = lax.axis_size("seq")
    bit = 1
    comes = []
    while bit < count:
        batch, source, inner, target, rest, channels = value.shape
        split = value.reshape(batch, source, inner, target // 2, 2, rest, channels)
        mine = (number // bit) % 2
        keep = pick(split, mine, 4)
        come = seq_swap(pick(split, 1 - mine, 4), bit)
        comes.append(come)
        first = jnp.where(mine == 0, keep, come)
        second = jnp.where(mine == 0, come, keep)
        value = jnp.stack([first, second], axis=1).reshape(
            batch, 2 * source, inner, target // 2, rest, channels
        )
        bit *= 2
    return value[:, :, :, 0], comes


def to_residues(value, number):
    batch, rows, channels = value.shape
    count = lax.axis_size("seq")
    value = value.reshape(batch, 1, rows // BASE_DILATION, count, BASE_DILATION // count, channels)
    return exchange(value, number)[0].reshape(batch, rows, channels)


def from_residues(value, number):
    batch, rows, channels = value.shape
    count = lax.axis_size("seq")
    own = BASE_DILATION // count
    inner = rows // BASE_DILATION
    value = value.reshape(batch, 1, count, inner, own, channels).transpose(0, 1, 3, 2, 4, 5)
    value, comes = exchange(value, number)
    return value.transpose(0, 2, 1, 3, 4).reshape(batch, rows, channels), comes


def shifts(value, step):
    rows = value.shape[-2]
    width = 2 * step[1]
    pad = [(0, 0)] * (value.ndim - 2) + [(width, width), (0, 0)]
    padded = jnp.pad(value, pad)
    axis = value.ndim - 2
    return [
        lax.dynamic_slice_in_dim(padded, width - (tap - 1) * step[0], rows, axis) for tap in range(3)
    ]


def split_cores(section_inputs, cotangent, core, first, batch):
    rows, channels = cotangent.shape[2:]
    quarter = rows // 4
    blocks = rows // BASE_DILATION

    def kernel(core_ref, inputs_ref, top_ref, send_ref, keep_ref):
        low = core_ref[0] == 0
        for which, value in enumerate((inputs_ref[0, 0, 0], top_ref[0, 0])):
            value = value.astype(jnp.float32).reshape(blocks, 4, quarter // blocks, channels)
            for side in range(2):
                first_part = value[:, 2 * side].reshape(quarter, channels)
                second_part = value[:, 2 * side + 1].reshape(quarter, channels)
                keep = jnp.where(low, first_part, second_part)
                send = jnp.where(low, second_part, first_part)
                keep_ref[which, side] = keep.astype(keep_ref.dtype)
                send_ref[which, side] = send.astype(send_ref.dtype)

    out = jax.ShapeDtypeStruct((2 * batch, 2, quarter, channels), cotangent.dtype)
    part = pl.BlockSpec((2, 2, quarter, channels), lambda m: (m, 0, 0, 0))
    return pl.pallas_call(
        kernel,
        grid=(batch,),
        in_specs=[
            pl.BlockSpec(memory_space=pltpu.SMEM),
            pl.BlockSpec((1, 1, 1, rows, channels), lambda m: (0, first + m, 0, 0, 0)),
            pl.BlockSpec((1, 1, rows, channels), lambda m: (first + m, 0, 0, 0)),
        ],
        out_specs=[part, part],
        out_shape=[out, out],
        compiler_params=pltpu.CompilerParams(vmem_limit_bytes=16 * 2**20),
        cost_estimate=pl.CostEstimate(
            flops=0, bytes_accessed=8 * batch * rows * channels, transcendentals=0
        ),
    )(core.reshape(1).astype(jnp.int32), section_inputs, cotangent)


def after(value, *events):
    return lax.optimization_barrier((value,) + events)[0]


def choose(flag, first, second):
    return jnp.where(flag, first, second)


def on_device(
    section_inputs,
    cotangent,
    conv_weight,
    out_weight,
    norm_scale,
    norm_shift,
    inner_scale,
    inner_shift,
):
    sections = lax.axis_size("section")
    windows = lax.axis_size("dp")
    count = lax.axis_size("seq")
    section = lax.axis_index("section")
    number = lax.axis_index("seq")
    window = lax.axis_index("dp")
    inputs = section_inputs[0, :, 0]
    top = cotangent[:, 0]
    micro, rows, channels = inputs.shape
    kernel = conv_weight[0]
    inner = kernel.shape[2]
    kernel_flat = kernel.reshape(3 * channels, inner)
    out_w = out_weight[0]
    own = BASE_DILATION // count
    step = (own * (1 + section % 2), own)
    gathered = count == 4 and windows == 2
    core, side = number % 2, number // 2
    ticks = micro + LAG * (sections - 1)

    def send_down(value, now):
        hops = [hop for hop in range(sections - 1) if 0 <= now - LAG * hop < micro]
        return {
            hop: lax.ppermute(value, "section", [(sections - 1 - hop, sections - 2 - hop)])
            for hop in reversed(hops)
        }

    def receive(comes, *events):
        value = None
        for hop, come in comes.items():
            come = after(come, *events)
            events = (come,)
            value = come if value is None else jnp.where(section == sections - 2 - hop, come, value)
        return value

    def forward(block_in):
        pre = block_in.astype(jnp.float32) * norm_scale[0] + norm_shift[0]
        act, slope = gelu_pair(pre)
        hidden = act.astype(jnp.bfloat16)
        up, same, down = shifts(hidden, step)
        taps = jnp.concatenate([down, same, up], axis=-1)
        inner_pre = (
            jnp.dot(taps, kernel_flat, preferred_element_type=jnp.float32) * inner_scale[0]
            + inner_shift[0]
        )
        inner_act, inner_slope = gelu_pair(inner_pre)
        return lax.optimization_barrier(
            (
                hidden,
                slope * norm_scale[0],
                inner_act.astype(jnp.bfloat16),
                inner_slope * inner_scale[0],
            )
        )

    def transposed(unit):
        return lax.optimization_barrier(
            jnp.concatenate(
                [
                    lax.dot_general(
                        unit,
                        kernel[tap],
                        (((1,), (1,)), ((), ())),
                        preferred_element_type=jnp.float32,
                    ).astype(jnp.bfloat16)
                    for tap in range(3)
                ]
            )
        )

    if count == 4:

        def swap_sides(keep, come):
            send = jnp.stack([pick(keep, 1 - side, 1), pick(come, 1 - side, 1)], 1)
            mine = jnp.stack([pick(keep, side, 1), pick(come, side, 1)], 1)
            return send, mine

        def settle(mine, come):
            mine, come = (
                jnp.stack(
                    [
                        choose(core == 0, one[:, 0], one[:, 1]),
                        choose(core == 0, one[:, 1], one[:, 0]),
                    ],
                    1,
                )
                for one in (mine, come)
            )
            both = jnp.stack([choose(side == 0, mine, come), choose(side == 0, come, mine)], 1)
            both = both.reshape(-1, rows, channels)
            return both[0], both[1]

        send, keep = split_cores(section_inputs[:, :1], cotangent[:1], core, 0, 1)
        come = seq_swap(send, 1)
        later_core = after(core, send)
        later_send, later_keep = split_cores(section_inputs, cotangent, later_core, 1, micro - 1)
        later_come = seq_swap(later_send, 1)
        send, mine = swap_sides(keep, come)
        come = seq_swap(send, 2)
        later_keep = after(later_keep, send)
        later_send, later_mine = swap_sides(later_keep, later_come)
        parts = [later_send[2 * m : 2 * m + 2] for m in range(micro - 1)]
        parts = lax.optimization_barrier(tuple(parts) + (later_mine,))
        later_mine = parts[-1]
        back_kernel = transposed(after(jnp.eye(inner, dtype=jnp.bfloat16), *parts))
        come = after(come, *parts)
        arriving = [(mine, come)]

        def arrived(m, *events):
            mine, come = arriving[m]
            if m + 1 < micro:
                send = parts[m] if m == 0 else after(parts[m], *events)
                arriving.append((later_mine[2 * m : 2 * m + 2], seq_swap(send, 2)))
            return settle(mine, after(come, *events))
    else:
        swapped = to_residues(jnp.concatenate([inputs, top]), number)
        back_kernel = kernel.transpose(0, 2, 1).reshape(3 * inner, channels)

        def arrived(m, *events):
            return swapped[m], swapped[micro + m]

    tops, hidden, slope, inner_act, inner_slope = [], [], [], [], []

    def tick(index, received):
        def of_index(values):
            value = values[0]
            for m in range(1, len(values)):
                value = jnp.where(index >= m, values[m], value)
            return value

        grad_top = of_index(tops)
        if received is not None:
            grad_top = jnp.where(section == sections - 1, grad_top, received)
        grad_inner = lax.dot_general(
            grad_top, out_w, (((1,), (1,)), ((), ())), preferred_element_type=jnp.float32
        )
        grad_conv = (grad_inner * of_index(inner_slope)).astype(jnp.bfloat16)
        back = jnp.concatenate(shifts(grad_conv, step), axis=-1)
        grad_hidden = jnp.dot(back, back_kernel, preferred_element_type=jnp.float32)
        grad_block = (grad_top.astype(jnp.float32) + grad_hidden * of_index(slope)).astype(
            jnp.bfloat16
        )
        return lax.optimization_barrier((grad_top, grad_conv, grad_block))

    def of_section(m, which):
        value = done[m][which]
        for below in range(1, sections):
            value = jnp.where(
                section == sections - 1 - below, done[m + LAG * below][which], value
            )
        return value

    def exchange_rows(value, far_value):
        return jnp.concatenate(
            [choose(window == 0, value, far_value), choose(window == 0, far_value, value)]
        )

    half = channels // 2
    share = half // 2
    sent, done = [], []
    near_hidden, far_hidden = [], []
    near_grad, far_grad = [None] * micro, [None] * micro
    conv_total = 0.0
    out_part = 0.0
    for now in range(ticks):
        if now < micro:
            block_in, one_top = arrived(now, *([done[now - 1]] if now else []))
            one = forward(block_in)
            tops.append(one_top)
            hidden.append(one[0])
            slope.append(one[1])
            inner_act.append(one[2])
            inner_slope.append(one[3])
        received = None
        if now >= LAG:
            events = [done[now - 1]]
            if now < micro:
                events.append(hidden[now])
            if gathered and now == NEAR:
                events.append(near_hidden)
            if gathered and now == FAR:
                events.append(far_hidden)
            if gathered and now == ticks - 1:
                events += [near_grad[0], comes_early[0]]
            received = receive(sent[now - LAG], *events)
        done.append(tick(now - LAG * (sections - 1 - section), received))
        if now + LAG < ticks:
            sent.append(send_down(done[now][2], now))
        if gathered and now == micro - 1:
            wide = jnp.concatenate(after(tuple(hidden), done[now]))
            mine = choose(side == 0, wide[:, :half], wide[:, half:])
            other = choose(side == 0, wide[:, half:], wide[:, :half])
            near_hidden = (mine, seq_swap(other, 2))
        if gathered and now == micro:
            near_hidden = jnp.concatenate(
                [one.reshape(micro, rows, half) for one in after(near_hidden, done[now])], axis=1
            )
            far_hidden = dp_swap(near_hidden)
        m = now - LAG * (sections - 1)
        if m >= 0:
            out_part = out_part + lax.dot_general(
                of_section(m, 0),
                inner_act[m],
                (((0,), (0,)), ((), ())),
                preferred_element_type=jnp.float32,
            )
        if gathered and m >= 0:
            grad_conv = of_section(m, 1)
            near_grad[m] = (grad_conv, seq_swap(grad_conv, 2))
        if gathered and m >= 1:
            near_grad[m - 1] = jnp.concatenate(after(near_grad[m - 1], done[now]))
            far_grad[m - 1] = dp_swap(near_grad[m - 1])
        if gathered and m == micro - 2:
            early = jnp.stack([of_section(one, 2) for one in range(micro - 1)])
            early, comes_early = from_residues(early, number)

    def add_conv(total, m, *events):
        if gathered:
            all_hidden = exchange_rows(near_hidden[m], far_hidden[m])
            all_grad = exchange_rows(near_grad[m], after(far_grad[m], *events))
            all_grad = all_grad.reshape(4, rows, inner)
            back = jnp.concatenate(shifts(all_grad, step), axis=-1).reshape(4 * rows, 3 * inner)
        else:
            all_hidden = hidden[m]
            back = jnp.concatenate(shifts(of_section(m, 1), step), axis=-1)
        return total + lax.dot_general(
            all_hidden, back, (((0,), (0,)), ((), ())), preferred_element_type=jnp.float32
        )

    if gathered:
        out_part = after(out_part, near_grad[1])
        quarters = out_part.reshape(2, 2, share, inner)
        keep = choose(core == 0, quarters[:, 0], quarters[:, 1])
        send = choose(core == 0, quarters[:, 1], quarters[:, 0]).astype(jnp.bfloat16)
        come_out = seq_swap(send, 1)
        come_out = after(come_out, near_grad[1]).astype(jnp.float32)
        columns = [keep[0] + come_out[0], keep[1] + come_out[1]]
        send = choose(side == 0, columns[1], columns[0]).astype(jnp.bfloat16)
        keep = choose(side == 0, columns[0], columns[1])
        come = seq_swap(send, 2)
        near_grad[-1] = jnp.concatenate(after(near_grad[-1], send))
        far_grad[-1] = dp_swap(near_grad[-1])
        far_grad[-2] = after(far_grad[-2], near_grad[-1])
        late = after(of_section(micro - 1, 2)[None], send)
        late, comes_late = from_residues(late, number)
        grads_out = jnp.concatenate([early, late])
        for m in range(micro - 1):
            events = [send] if m == 0 else [send, comes_early[-1]]
            conv_total = lax.optimization_barrier(add_conv(conv_total, m, *events))
        come = after(come, conv_total)
        columns = (keep + come.astype(jnp.float32)).astype(jnp.bfloat16)
        come_out = dp_swap(columns)
        conv_total = add_conv(conv_total, micro - 1, columns)
    else:
        for m in range(micro):
            conv_total = add_conv(conv_total, m)
        grads_out, _ = from_residues(jnp.stack([of_section(m, 2) for m in range(micro)]), number)

    factor = 1.0 / float(micro * windows)
    if gathered:
        low, high = conv_total[:share], conv_total[share:]
        come = seq_swap(choose(core == 0, high, low).astype(jnp.bfloat16), 1)
        come = after(come, comes_late[-1])
        conv_sum = choose(core == 0, low, high) + come.astype(jnp.float32)
        conv_sum = jnp.stack([conv_sum[:, k * inner : (k + 1) * inner] for k in range(3)])
        conv_sum = conv_sum * factor
        come_out = after(come_out, conv_sum)
        out_sum = (columns.astype(jnp.float32) + come_out.astype(jnp.float32)).T
    else:
        out_part = out_part.T
        conv_part = conv_total.reshape(channels, 3, inner).transpose(1, 0, 2)
        conv_sum, out_sum = (
            lax.psum(
                lax.psum_scatter(part.astype(jnp.bfloat16), "seq", scatter_dimension=1, tiled=True),
                "dp",
            ).astype(jnp.float32)
            for part in (conv_part, out_part)
        )
        conv_sum = conv_sum * factor
    return (
        grads_out.reshape(section_inputs.shape),
        conv_sum[None],
        (out_sum * factor)[None],
    )


def solution(mesh):
    return jax.shard_map(
        on_device,
        mesh=mesh,
        in_specs=(
            P("section", None, "dp", "seq", None),
            P(None, "dp", "seq", None),
            P("section", None, None, None),
            P("section", None, None),
            P("section", None),
            P("section", None),
            P("section", None),
            P("section", None),
        ),
        out_specs=(
            P("section", None, "dp", "seq", None),
            P("section", None, "seq", None),
            P("section", None, "seq"),
        ),
        check_vma=False,
    )
```

```python
import jax
import jax.numpy as jnp
from jax import lax
from jax.experimental import pallas as pl
from jax.experimental.pallas import tpu as pltpu
from jax.sharding import PartitionSpec as P

BASE_DILATION = 32
LAG = 2
NEAR = 5
FAR = 8


gelu_coeff = 0.7978845608028654
cubic_coeff = 0.044715


def gelu_pair(inputs):
    squared = inputs * inputs
    inner_arg = gelu_coeff * (inputs + cubic_coeff * inputs * squared)
    tanh_val = jnp.tanh(inner_arg)
    result = 0.5 * inputs * (1.0 + tanh_val)
    slope_val = 0.5 * (1.0 + tanh_val) + 0.5 * inputs * (1.0 - tanh_val * tanh_val) * gelu_coeff * (
        1.0 + 3.0 * cubic_coeff * squared
    )
    return (result, slope_val)


def seq_swap(value, bit):
    count = lax.axis_size("seq")
    return lax.ppermute(value, "seq", [(i, i ^ bit) for i in range(count)])


def dp_swap(value):
    return lax.ppermute(value, "dp", [(0, 1), (1, 0)])


def pick(value, index, axis):
    return lax.dynamic_index_in_dim(value, index, axis, keepdims=False)


def exchange(value, number):
    count = lax.axis_size("seq")
    bit = 1
    comes = []
    while bit < count:
        batch, source, inner, target, rest, channels = value.shape
        split = value.reshape(batch, source, inner, target // 2, 2, rest, channels)
        mine = (number // bit) % 2
        keep = pick(split, mine, 4)
        come = seq_swap(pick(split, 1 - mine, 4), bit)
        comes.append(come)
        first = jnp.where(mine == 0, keep, come)
        second = jnp.where(mine == 0, come, keep)
        value = jnp.stack([first, second], axis=1).reshape(
            batch, 2 * source, inner, target // 2, rest, channels
        )
        bit *= 2
    return value[:, :, :, 0], comes


def to_residues(value, number):
    batch, rows, channels = value.shape
    count = lax.axis_size("seq")
    value = value.reshape(batch, 1, rows // BASE_DILATION, count, BASE_DILATION // count, channels)
    return exchange(value, number)[0].reshape(batch, rows, channels)


def from_residues(value, number):
    batch, rows, channels = value.shape
    count = lax.axis_size("seq")
    own = BASE_DILATION // count
    inner = rows // BASE_DILATION
    value = value.reshape(batch, 1, count, inner, own, channels).transpose(0, 1, 3, 2, 4, 5)
    value, comes = exchange(value, number)
    return value.transpose(0, 2, 1, 3, 4).reshape(batch, rows, channels), comes


def shifts(value, step):
    rows = value.shape[-2]
    width = 2 * step[1]
    pad = [(0, 0)] * (value.ndim - 2) + [(width, width), (0, 0)]
    padded = jnp.pad(value, pad)
    axis = value.ndim - 2
    return [
        lax.dynamic_slice_in_dim(padded, width - (tap - 1) * step[0], rows, axis) for tap in range(3)
    ]


def split_cores(section_inputs, cotangent, core, first, batch):
    rows, channels = cotangent.shape[2:]
    quarter = rows // 4
    blocks = rows // BASE_DILATION

    def kernel(core_ref, inputs_ref, top_ref, send_ref, keep_ref):
        low = core_ref[0] == 0
        for which, value in enumerate((inputs_ref[0, 0, 0], top_ref[0, 0])):
            value = value.astype(jnp.float32).reshape(blocks, 4, quarter // blocks, channels)
            for side in range(2):
                first_part = value[:, 2 * side].reshape(quarter, channels)
                second_part = value[:, 2 * side + 1].reshape(quarter, channels)
                keep = jnp.where(low, first_part, second_part)
                send = jnp.where(low, second_part, first_part)
                keep_ref[which, side] = keep.astype(keep_ref.dtype)
                send_ref[which, side] = send.astype(send_ref.dtype)

    out = jax.ShapeDtypeStruct((2 * batch, 2, quarter, channels), cotangent.dtype)
    part = pl.BlockSpec((2, 2, quarter, channels), lambda m: (m, 0, 0, 0))
    return pl.pallas_call(
        kernel,
        grid=(batch,),
        in_specs=[
            pl.BlockSpec(memory_space=pltpu.SMEM),
            pl.BlockSpec((1, 1, 1, rows, channels), lambda m: (0, first + m, 0, 0, 0)),
            pl.BlockSpec((1, 1, rows, channels), lambda m: (first + m, 0, 0, 0)),
        ],
        out_specs=[part, part],
        out_shape=[out, out],
        compiler_params=pltpu.CompilerParams(vmem_limit_bytes=16 * 2**20),
        cost_estimate=pl.CostEstimate(
            flops=0, bytes_accessed=8 * batch * rows * channels, transcendentals=0
        ),
    )(core.reshape(1).astype(jnp.int32), section_inputs, cotangent)


def after(value, *events):
    return lax.optimization_barrier((value,) + events)[0]


def choose(flag, first, second):
    return jnp.where(flag, first, second)


def on_device(
    section_inputs,
    cotangent,
    conv_weight,
    out_weight,
    norm_scale,
    norm_shift,
    inner_scale,
    inner_shift,
):
    sections = lax.axis_size("section")
    windows = lax.axis_size("dp")
    count = lax.axis_size("seq")
    section = lax.axis_index("section")
    number = lax.axis_index("seq")
    window = lax.axis_index("dp")
    inputs = section_inputs[0, :, 0]
    top = cotangent[:, 0]
    micro, rows, channels = inputs.shape
    kernel = conv_weight[0]
    inner = kernel.shape[2]
    kernel_flat = kernel.reshape(3 * channels, inner)
    out_w = out_weight[0]
    own = BASE_DILATION // count
    step = (own * (1 + section % 2), own)
    gathered = count == 4 and windows == 2
    core, side = number % 2, number // 2
    ticks = micro + LAG * (sections - 1)

    def send_down(value, now):
        hops = [hop for hop in range(sections - 1) if 0 <= now - LAG * hop < micro]
        return {
            hop: lax.ppermute(value, "section", [(sections - 1 - hop, sections - 2 - hop)])
            for hop in reversed(hops)
        }

    def receive(comes, *events):
        value = None
        for hop, come in comes.items():
            come = after(come, *events)
            events = (come,)
            value = come if value is None else jnp.where(section == sections - 2 - hop, come, value)
        return value

    def forward(block_in):
        pre = block_in.astype(jnp.float32) * norm_scale[0] + norm_shift[0]
        act, slope = gelu_pair(pre)
        hidden = act.astype(jnp.bfloat16)
        up, same, down = shifts(hidden, step)
        taps = jnp.concatenate([down, same, up], axis=-1)
        inner_pre = (
            jnp.dot(taps, kernel_flat, preferred_element_type=jnp.float32) * inner_scale[0]
            + inner_shift[0]
        )
        inner_act, inner_slope = gelu_pair(inner_pre)
        return lax.optimization_barrier(
            (
                hidden,
                slope * norm_scale[0],
                inner_act.astype(jnp.bfloat16),
                inner_slope * inner_scale[0],
            )
        )

    def transposed(unit):
        return lax.optimization_barrier(
            jnp.concatenate(
                [
                    lax.dot_general(
                        unit,
                        kernel[tap],
                        (((1,), (1,)), ((), ())),
                        preferred_element_type=jnp.float32,
                    ).astype(jnp.bfloat16)
                    for tap in range(3)
                ]
            )
        )

    if count == 4:

        def swap_sides(keep, come):
            send = jnp.stack([pick(keep, 1 - side, 1), pick(come, 1 - side, 1)], 1)
            mine = jnp.stack([pick(keep, side, 1), pick(come, side, 1)], 1)
            return send, mine

        def settle(mine, come):
            mine, come = (
                jnp.stack(
                    [
                        choose(core == 0, one[:, 0], one[:, 1]),
                        choose(core == 0, one[:, 1], one[:, 0]),
                    ],
                    1,
                )
                for one in (mine, come)
            )
            both = jnp.stack([choose(side == 0, mine, come), choose(side == 0, come, mine)], 1)
            both = both.reshape(-1, rows, channels)
            return both[0], both[1]

        send, keep = split_cores(section_inputs, cotangent, core, 0, 1)
        come = seq_swap(send, 1)
        later_core = after(core, send)
        later_send, later_keep = split_cores(section_inputs, cotangent, later_core, 1, micro - 1)
        later_come = seq_swap(later_send, 1)
        send, mine = swap_sides(keep, come)
        come = seq_swap(send, 2)
        later_keep = after(later_keep, send)
        later_send, later_mine = swap_sides(later_keep, later_come)
        parts = [later_send[2 * m : 2 * m + 2] for m in range(micro - 1)]
        parts = lax.optimization_barrier(tuple(parts) + (later_mine,))
        later_mine = parts[-1]
        back_kernel = transposed(after(jnp.eye(inner, dtype=jnp.bfloat16), *parts))
        come = after(come, *parts)
        arriving = [(mine, come)]

        def arrived(m, *events):
            mine, come = arriving[m]
            if m + 1 < micro:
                send = parts[m] if m == 0 else after(parts[m], *events)
                arriving.append((later_mine[2 * m : 2 * m + 2], seq_swap(send, 2)))
            return settle(mine, after(come, *events))
    else:
        swapped = to_residues(jnp.concatenate([inputs, top]), number)
        back_kernel = kernel.transpose(0, 2, 1).reshape(3 * inner, channels)

        def arrived(m, *events):
            return swapped[m], swapped[micro + m]

    tops, hidden, slope, inner_act, inner_slope = [], [], [], [], []

    def tick(index, received):
        def of_index(values):
            value = values[0]
            for m in range(1, len(values)):
                value = jnp.where(index >= m, values[m], value)
            return value

        grad_top = of_index(tops)
        if received is not None:
            grad_top = jnp.where(section == sections - 1, grad_top, received)
        grad_inner = lax.dot_general(
            grad_top, out_w, (((1,), (1,)), ((), ())), preferred_element_type=jnp.float32
        )
        grad_conv = (grad_inner * of_index(inner_slope)).astype(jnp.bfloat16)
        back = jnp.concatenate(shifts(grad_conv, step), axis=-1)
        grad_hidden = jnp.dot(back, back_kernel, preferred_element_type=jnp.float32)
        grad_block = (grad_top.astype(jnp.float32) + grad_hidden * of_index(slope)).astype(
            jnp.bfloat16
        )
        return lax.optimization_barrier((grad_top, grad_conv, grad_block))

    def of_section(m, which):
        value = done[m][which]
        for below in range(1, sections):
            value = jnp.where(
                section == sections - 1 - below, done[m + LAG * below][which], value
            )
        return value

    def exchange_rows(value, far_value):
        return jnp.concatenate(
            [choose(window == 0, value, far_value), choose(window == 0, far_value, value)]
        )

    half = channels // 2
    share = half // 2
    sent, done = [], []
    near_hidden, far_hidden = [], []
    near_grad, far_grad = [None] * micro, [None] * micro
    conv_total = 0.0
    out_part = 0.0
    for now in range(ticks):
        if now < micro:
            block_in, one_top = arrived(now, *([done[now - 1]] if now else []))
            one = forward(block_in)
            tops.append(one_top)
            hidden.append(one[0])
            slope.append(one[1])
            inner_act.append(one[2])
            inner_slope.append(one[3])
        received = None
        if now >= LAG:
            events = [done[now - 1]]
            if now < micro:
                events.append(hidden[now])
            if gathered and now == NEAR:
                events.append(near_hidden)
            if gathered and now == FAR:
                events.append(far_hidden)
            if gathered and now == ticks - 1:
                events += [near_grad[0], comes_early[0]]
            received = receive(sent[now - LAG], *events)
        done.append(tick(now - LAG * (sections - 1 - section), received))
        if now + LAG < ticks:
            sent.append(send_down(done[now][2], now))
        if gathered and now == micro - 1:
            wide = jnp.concatenate(after(tuple(hidden), done[now]))
            mine = choose(side == 0, wide[:, :half], wide[:, half:])
            other = choose(side == 0, wide[:, half:], wide[:, :half])
            near_hidden = (mine, seq_swap(other, 2))
        if gathered and now == micro:
            near_hidden = jnp.concatenate(
                [one.reshape(micro, rows, half) for one in after(near_hidden, done[now])], axis=1
            )
            far_hidden = dp_swap(near_hidden)
        m = now - LAG * (sections - 1)
        if m >= 0:
            out_part = out_part + lax.dot_general(
                of_section(m, 0),
                inner_act[m],
                (((0,), (0,)), ((), ())),
                preferred_element_type=jnp.float32,
            )
        if gathered and m >= 0:
            grad_conv = of_section(m, 1)
            near_grad[m] = (grad_conv, seq_swap(grad_conv, 2))
        if gathered and m >= 1:
            near_grad[m - 1] = jnp.concatenate(after(near_grad[m - 1], done[now]))
            far_grad[m - 1] = dp_swap(near_grad[m - 1])
        if gathered and m == micro - 2:
            early = jnp.stack([of_section(one, 2) for one in range(micro - 1)])
            early, comes_early = from_residues(early, number)

    def add_conv(total, m, *events):
        if gathered:
            all_hidden = exchange_rows(near_hidden[m], far_hidden[m])
            all_grad = exchange_rows(near_grad[m], after(far_grad[m], *events))
            all_grad = all_grad.reshape(4, rows, inner)
            back = jnp.concatenate(shifts(all_grad, step), axis=-1).reshape(4 * rows, 3 * inner)
        else:
            all_hidden = hidden[m]
            back = jnp.concatenate(shifts(of_section(m, 1), step), axis=-1)
        return total + lax.dot_general(
            all_hidden, back, (((0,), (0,)), ((), ())), preferred_element_type=jnp.float32
        )

    if gathered:
        out_part = after(out_part, near_grad[1])
        quarters = out_part.reshape(2, 2, share, inner)
        keep = choose(core == 0, quarters[:, 0], quarters[:, 1])
        send = choose(core == 0, quarters[:, 1], quarters[:, 0]).astype(jnp.bfloat16)
        come_out = seq_swap(send, 1)
        come_out = after(come_out, near_grad[1]).astype(jnp.float32)
        columns = [keep[0] + come_out[0], keep[1] + come_out[1]]
        send = choose(side == 0, columns[1], columns[0]).astype(jnp.bfloat16)
        keep = choose(side == 0, columns[0], columns[1])
        come = seq_swap(send, 2)
        near_grad[-1] = jnp.concatenate(after(near_grad[-1], send))
        far_grad[-1] = dp_swap(near_grad[-1])
        far_grad[-2] = after(far_grad[-2], near_grad[-1])
        late = after(of_section(micro - 1, 2)[None], send)
        late, comes_late = from_residues(late, number)
        grads_out = jnp.concatenate([early, late])
        for m in range(micro - 1):
            events = [send] if m == 0 else [send, comes_early[-1]]
            conv_total = lax.optimization_barrier(add_conv(conv_total, m, *events))
        come = after(come, conv_total)
        columns = (keep + come.astype(jnp.float32)).astype(jnp.bfloat16)
        come_out = dp_swap(columns)
        conv_total = add_conv(conv_total, micro - 1, columns, comes_late[0])
    else:
        for m in range(micro):
            conv_total = add_conv(conv_total, m)
        grads_out, _ = from_residues(jnp.stack([of_section(m, 2) for m in range(micro)]), number)

    factor = 1.0 / float(micro * windows)
    if gathered:
        low, high = conv_total[:share], conv_total[share:]
        come = seq_swap(choose(core == 0, high, low).astype(jnp.bfloat16), 1)
        come = after(come, comes_late[-1])
        conv_sum = choose(core == 0, low, high) + come.astype(jnp.float32)
        conv_sum = jnp.stack([conv_sum[:, k * inner : (k + 1) * inner] for k in range(3)])
        conv_sum = conv_sum * factor
        come_out = after(come_out, conv_sum)
        out_sum = (columns.astype(jnp.float32) + come_out.astype(jnp.float32)).T
    else:
        out_part = out_part.T
        conv_part = conv_total.reshape(channels, 3, inner).transpose(1, 0, 2)
        conv_sum, out_sum = (
            lax.psum(
                lax.psum_scatter(part.astype(jnp.bfloat16), "seq", scatter_dimension=1, tiled=True),
                "dp",
            ).astype(jnp.float32)
            for part in (conv_part, out_part)
        )
        conv_sum = conv_sum * factor
    return (
        grads_out.reshape(section_inputs.shape),
        conv_sum[None],
        (out_sum * factor)[None],
    )


def solution(mesh):
    return jax.shard_map(
        on_device,
        mesh=mesh,
        in_specs=(
            P("section", None, "dp", "seq", None),
            P(None, "dp", "seq", None),
            P("section", None, None, None),
            P("section", None, None),
            P("section", None),
            P("section", None),
            P("section", None),
            P("section", None),
        ),
        out_specs=(
            P("section", None, "dp", "seq", None),
            P("section", None, "seq", None),
            P("section", None, "seq"),
        ),
        check_vma=False,
    )
```
